256 devices in a mesh: row: 64 (over y, z, core), col: 4 (over x).
Axes of the slice: x: 4, y: 4, z: 8, core: 2. Of those that a mesh axis runs over, the one named last changes fastest.
Arguments:
- features: bfloat16 [65536, 128], P(('col', 'row')), may hold values from -6 to 6
- weight: bfloat16 [128, 128], replicated, may hold values from -0.5 to 0.5
- bias: float32 [128], replicated, may hold values from -3 to 3
- block_values: bfloat16 [64, 4, 320, 128, 128], P('row', 'col'), may hold values from -0.078125 to 0.078125
- block_rows: int32 [64, 4, 320], P('row', 'col'), may hold values from 0 to 7
- block_cols: int32 [64, 4, 320], P('row', 'col'), may hold values from 0 to 127
- block_counts: int32 [64, 4], P('row', 'col'), may hold values from 40 to 320, as said below
- cotangent: bfloat16 [65536, 128], P(('row', 'col')), may hold values from -6 to 6
Outputs:
- activated: bfloat16 [65536, 128], P(('row', 'col'))
- feature_grad: float32 [65536, 128], P(('col', 'row'))
- weight_grad: float32 [128, 128], replicated
- bias_grad: float32 [128], replicated
The draws below stay inside these ranges and needn't reach their ends.
Inputs may be any that keep to these rules, and one draw needn't show every extreme that they name: `block_rows`: block-row of a slot inside its row group. `block_cols`: block-column of a slot inside its column group. `block_counts`: slots from this count on hold no block and are ignored; some device holds exactly 320.
All inputs are finite; a program needn't handle non-finite values.
Results may differ from the reference program's by a relative error of at most 0.009.
Values may be sent and summed in bfloat16 or wider, within the bound.
No kernel may reach another device: no remote copies, remote signals or barrier semaphores. Data moves between devices by JAX's collectives and lax.ppermute only.
A program may use at most 128 MiB of HBM per device.

```python
import jax
import jax.numpy as jnp
from jax import lax

F = 128
BLK = 128
NODE_DEV = 256
KMAX = 320
N_NODES = 65536
RB = 8
CB = 128
N_ROW = 64
N_COL = 4


def draw_block_counts(key, part):
    key = jax.random.fold_in(key, 7)
    base_key, busy_key = jax.random.split(key)
    base = jax.random.randint(base_key, (N_ROW * N_COL,), KMAX // 8, KMAX // 2 + 1)
    busiest = jax.random.randint(busy_key, (4,), 0, N_ROW * N_COL)
    filled = base.at[busiest].set(KMAX)
    return filled.reshape(N_ROW, N_COL).astype(jnp.int32)


def set_ends(array, stream_key, low, high):
    longest = array.shape.index(max(array.shape))
    spots = []
    for shift in (0, 1):
        where = [jax.random.randint(jax.random.fold_in(stream_key, axis), (), 0, length) for axis, length in enumerate(array.shape)]
        where[longest] = (where[longest] + shift) % array.shape[longest]
        spots.append(tuple(where))
    return array.at[spots[0]].set(low).at[spots[1]].set(high)


def block_scale(key, extent, pieces, least, largest):
    def one(dim, parts):
        draws = jax.random.uniform(jax.random.fold_in(jax.random.fold_in(key, 6), dim), (parts,), jnp.float32, least / len(pieces), largest / len(pieces))
        return jnp.repeat(jnp.exp(draws), extent[dim] // parts).reshape((-1,) + (1,) * (len(extent) - dim - 1))

    level = one(*pieces[0])
    for cut in pieces[1:]:
        level = level * one(*cut)
    return level


def scatter_about(key, extent, deviation, bound, cuts=(), kind=jnp.bfloat16):
    result = jax.random.normal(key, extent, jnp.float32) * deviation
    if len(cuts) > 0:
        result = block_scale(key, extent, cuts, -0.22, 0.18) * result
    return jnp.clip(result, min=-bound, max=bound).astype(kind)


def setup_inputs(seed: int = 0) -> dict:
    arg_keys = jax.random.split(jax.random.key(seed), 9)
    return {
        "features": scatter_about(arg_keys[0], (N_NODES, F), 1.0, 6.0, ((0, 256),)),
        "weight": scatter_about(arg_keys[1], (F, F), F ** -0.5, 0.5),
        "bias": scatter_about(arg_keys[2], (F,), 0.5, 3.0, (), jnp.float32),
        "block_values": scatter_about(arg_keys[3], (N_ROW, N_COL, KMAX, BLK, BLK), (BLK * BLK * KMAX // (3 * NODE_DEV)) ** -0.5, 0.078125, ((0, 64), (1, 4))),
        "block_rows": set_ends(jax.random.randint(arg_keys[4], (N_ROW, N_COL, KMAX), 0, RB), jax.random.fold_in(arg_keys[4], 1), 0, RB - 1).astype(jnp.int32),
        "block_cols": set_ends(jax.random.randint(arg_keys[5], (N_ROW, N_COL, KMAX), 0, CB), jax.random.fold_in(arg_keys[5], 1), 0, CB - 1).astype(jnp.int32),
        "block_counts": draw_block_counts(jax.random.fold_in(arg_keys[8], 71), 0),
        "cotangent": scatter_about(arg_keys[7], (N_NODES, F), 1.0, 6.0, ((0, 256),)),
    }


def activation(value):
    return jax.nn.gelu(value, approximate=True)

def reference(features, weight, bias, block_values, block_rows, block_cols, block_counts, cotangent):
    width = features.shape[1]
    slot_index = jnp.arange(KMAX)
    column_blocks = features.reshape(N_COL, CB, BLK, width)

    def row_group(group):
        total = jnp.zeros((RB, BLK, width), jnp.float32)
        for column in range(N_COL):
            occupied = (slot_index < block_counts[group, column]).astype(jnp.float32)[:, None, None]
            picked = column_blocks[column][block_cols[group, column]]
            product = jnp.einsum('kab,kbf->kaf', block_values[group, column].astype(jnp.float32), picked.astype(jnp.float32), precision=lax.Precision.HIGHEST) * occupied
            total = total + jax.ops.segment_sum(product, block_rows[group, column], num_segments=RB)
        return total
    aggregated = lax.map(row_group, jnp.arange(N_ROW)).reshape(N_NODES, width).astype(jnp.bfloat16)
    pre = jnp.dot(aggregated, weight, preferred_element_type=jnp.float32) + bias
    activated = activation(pre).astype(jnp.bfloat16)
    _, backward = jax.vjp(activation, pre)
    pre_grad = backward(cotangent.astype(jnp.float32))[0].astype(jnp.bfloat16)
    scale = 1.0 / N_NODES ** 0.5
    weight_grad = lax.dot_general(aggregated, pre_grad, (((0,), (0,)), ((), ())), preferred_element_type=jnp.float32) * scale
    bias_grad = lax.optimization_barrier(jnp.sum(pre_grad.astype(jnp.float32), axis=0)) * scale
    hidden_grad = lax.dot_general(pre_grad, weight, (((1,), (1,)), ((), ())), preferred_element_type=jnp.float32).astype(jnp.bfloat16)
    row_blocks = hidden_grad.reshape(N_ROW, RB, BLK, width)

    def accumulate(carry, group):
        for column in range(N_COL):
            occupied = (slot_index < block_counts[group, column]).astype(jnp.float32)[:, None, None]
            picked = row_blocks[group][block_rows[group, column]]
            product = jnp.einsum('kab,kaf->kbf', block_values[group, column].astype(jnp.float32), picked.astype(jnp.float32), precision=lax.Precision.HIGHEST) * occupied
            carry = carry.at[column].add(jax.ops.segment_sum(product, block_cols[group, column], num_segments=CB))
        return (carry, None)
    start = jnp.zeros((N_COL, CB, BLK, width), jnp.float32)
    summed, _ = lax.scan(accumulate, start, jnp.arange(N_ROW))
    feature_grad = summed.reshape(N_NODES, width)
    return (activated, feature_grad, weight_grad, bias_grad)
```

```python
import math

import jax
import jax.numpy as jnp
import numpy as np
from jax import lax
from jax.experimental import pallas as pl
from jax.experimental.pallas import tpu as pltpu
from jax.sharding import PartitionSpec as P

BF = jnp.bfloat16
F32 = jnp.float32
NY, NZ, NC, NX = 4, 8, 2, 4
NROW = NY * NZ * NC
STEP = 16
GATHER_Z = ((0, 5, 3, 7), (4, 2, 1, 6))
SCATTER_Z = ((6, 1, 4, 0), (7, 2, 5, 3))
GATHER_PIECE = {(0, 0): 0, (0, 1): 1, (3, 0): 2, (1, 1): 3, (3, 1): 4, (1, 0): 5, (2, 0): 6, (2, 1): 7}

VMEM = pl.BlockSpec(memory_space=pltpu.VMEM)
SMEM = pl.BlockSpec(memory_space=pltpu.SMEM)


def place_tables():
    gather = np.zeros((NY, NZ), np.int32)
    scatter = np.zeros((NY, NZ), np.int32)
    for dy in range(NY):
        for half in range(2):
            for spot in range(4):
                gather[dy, GATHER_Z[half][spot]] = GATHER_PIECE[dy, half] * 8 + spot * 2
                scatter[dy, SCATTER_Z[half][spot]] = (dy * 2 + half) * 8 + spot * 2
    return gather.reshape(-1), scatter.reshape(-1)


def row_moves(dy=0, dz=0, flip_core=False):
    moves = []
    for y in range(NY):
        for z in range(NZ):
            for c in range(NC):
                to = (((y + dy) % NY) * NZ + (z + dz) % NZ) * NC + (c ^ int(flip_core))
                moves.append(((y * NZ + z) * NC + c, to))
    return moves


def send_y(value, step):
    return lax.ppermute(value, "row", row_moves(dy=step))


def send_z(value, step):
    return lax.ppermute(value, "row", row_moves(dz=step))


def send_core(value):
    return lax.ppermute(value, "row", row_moves(flip_core=True))


def send_x(value, step):
    return lax.ppermute(value, "col", [(i, (i + step) % NX) for i in range(NX)])


def cost(flops, size):
    return pl.CostEstimate(flops=flops, bytes_accessed=size, transcendentals=0)


def shape(dims, kind):
    return jax.ShapeDtypeStruct(dims, kind)


def partition_kernel(packed, count, own_list, other_list, totals):
    def visit(k, carry):
        own, other = carry
        word = packed[k]
        mine = word & 1

        @pl.when(mine == 1)
        def _():
            own_list[own] = word

        @pl.when(mine == 0)
        def _():
            other_list[other] = word

        return own + mine, other + 1 - mine

    own, other = lax.fori_loop(0, count[0], visit, (0, 0))
    spare = (8 << 10) | (64 << 20)
    for u in range(STEP):
        own_list[own + u] = spare
        other_list[other + u] = spare
    totals[0] = own
    totals[1] = other


def partition(packed, count):
    size = packed.shape[0] + STEP
    return pl.pallas_call(
        partition_kernel,
        out_shape=(shape((size,), jnp.int32), shape((size,), jnp.int32), shape((2,), jnp.int32)),
        in_specs=[SMEM, SMEM],
        out_specs=(SMEM, SMEM, SMEM),
        cost_estimate=cost(0, 1 << 20),
        name="partition",
    )(packed, count)


def slot_of(word):
    return (word >> 1) & 511


def row_of(word):
    return (word >> 10) & 15


def gather_of(word):
    return (word >> 14) & 63


def scatter_of(word):
    return (word >> 20) & 127


def forward_loop(which, slots, totals, values, held, total):
    def group(g, carry):
        for u in range(STEP):
            word = slots[g * STEP + u]
            total[row_of(word)] += jnp.dot(
                values[slot_of(word)], held[gather_of(word)], preferred_element_type=F32
            )
        return carry

    lax.fori_loop(0, (totals[which] + STEP - 1) // STEP, group, 0)


def forward_own_kernel(slots, totals, values, *rest):
    pieces, (out, held, total) = rest[:8], rest[8:]
    for p in range(8):
        held[pl.ds(p * 8, 8)] = pieces[p][...]
    total[...] = jnp.zeros_like(total)
    forward_loop(0, slots, totals, values, held, total)
    out[...] = total[0:8]


def forward_other_kernel(slots, totals, place, values, *rest):
    pieces, (before, keep, send1, send2, send3, held, total) = rest[:8], rest[8:]
    for p in range(8):
        held[pl.ds(p * 8, 8)] = pieces[p][...]
    total[0:8] = before[...]
    total[8] = jnp.zeros_like(total[8])
    forward_loop(1, slots, totals, values, held, total)
    x = place[0]
    keep[...] = total[pl.ds(2 * x, 2)]
    for step, send in ((1, send1), (2, send2), (3, send3)):
        send[...] = total[pl.ds(2 * lax.rem(x + step, NX), 2)].astype(BF)


def product_params():
    return pltpu.CompilerParams(vmem_limit_bytes=24 << 20)


def forward_own(slots, totals, values, pieces):
    return pl.pallas_call(
        forward_own_kernel,
        out_shape=shape((8, 128, 128), F32),
        in_specs=[SMEM, SMEM] + [VMEM] * 9,
        out_specs=VMEM,
        scratch_shapes=[pltpu.VMEM((64, 128, 128), BF), pltpu.VMEM((9, 128, 128), F32)],
        compiler_params=product_params(),
        cost_estimate=cost(1 << 31, 12 << 20),
        name="forward_own",
    )(slots, totals, values, *pieces)


def forward_other(slots, totals, place, values, pieces, before):
    part = (2, 128, 128)
    return pl.pallas_call(
        forward_other_kernel,
        out_shape=(shape(part, F32), shape(part, BF), shape(part, BF), shape(part, BF)),
        in_specs=[SMEM, SMEM, SMEM] + [VMEM] * 10,
        out_specs=(VMEM,) * 4,
        scratch_shapes=[pltpu.VMEM((64, 128, 128), BF), pltpu.VMEM((9, 128, 128), F32)],
        compiler_params=product_params(),
        cost_estimate=cost(1 << 31, 12 << 20),
        name="forward_other",
    )(slots, totals, place, values, *pieces, before)


def layer_kernel(keep, got1, got2, got3, weight, bias, cotangent, activated, hidden, terms):
    total = keep[...] + got1[...].astype(F32) + got2[...].astype(F32) + got3[...].astype(F32)
    aggregated = total.reshape(256, 128).astype(BF)
    w = weight[...]
    pre = jnp.dot(aggregated, w, preferred_element_type=F32) + bias[...]
    root = math.sqrt(2.0 / math.pi)
    square = pre * pre
    tanh = jnp.tanh(root * (pre + 0.044715 * (pre * square)))
    cdf = 0.5 * (1.0 + tanh)
    activated[...] = (pre * cdf).astype(BF)
    slope = cdf + 0.5 * pre * (1.0 - tanh * tanh) * (root * (1.0 + 3.0 * 0.044715 * square))
    pre_grad = (cotangent[...].astype(F32) * slope).astype(BF)
    terms[0:128] = lax.dot_general(
        aggregated, pre_grad, (((0,), (0,)), ((), ())), preferred_element_type=F32
    )
    bias_term = jnp.sum(pre_grad.astype(F32), axis=0, keepdims=True)
    terms[128:136] = jnp.broadcast_to(bias_term, (8, 128))
    for half in range(2):
        hidden[half] = lax.dot_general(
            w, pre_grad[half * 128 : half * 128 + 128], (((1,), (1,)), ((), ())),
            preferred_element_type=F32,
        ).astype(BF)


def layer(keep, got, weight, bias, cotangent):
    return pl.pallas_call(
        layer_kernel,
        out_shape=(shape((256, 128), BF), shape((2, 128, 128), BF), shape((136, 128), F32)),
        in_specs=[VMEM] * 7,
        out_specs=(VMEM,) * 3,
        cost_estimate=cost(1 << 26, 1 << 20),
        name="layer",
    )(keep, *got, weight, bias.reshape(1, 128), cotangent)


def backward_kernel(which, slots, totals, place, values, mine, got1, got2, got3, out, hidden, total):
    x = place[0]
    for step, part in ((0, mine), (1, got1), (2, got2), (3, got3)):
        hidden[pl.ds(2 * lax.rem(x + NX - step, NX), 2)] = part[...]
    hidden[8] = jnp.zeros_like(hidden[8])
    total[...] = jnp.zeros_like(total)

    def group(g, carry):
        for u in range(STEP):
            word = slots[g * STEP + u]
            total[scatter_of(word)] += jnp.dot(
                hidden[row_of(word)], values[slot_of(word)], preferred_element_type=F32
            )
        return carry

    lax.fori_loop(0, (totals[which] + STEP - 1) // STEP, group, 0)
    out[...] = total[0:64].astype(BF)


def backward(which, slots, totals, place, values, parts):
    def kernel(*refs):
        backward_kernel(which, *refs)

    return pl.pallas_call(
        kernel,
        out_shape=shape((64, 128, 128), BF),
        in_specs=[SMEM, SMEM, SMEM] + [VMEM] * 5,
        out_specs=VMEM,
        scratch_shapes=[pltpu.VMEM((9, 128, 128), BF), pltpu.VMEM((65, 128, 128), F32)],
        compiler_params=product_params(),
        cost_estimate=cost(1 << 31, 12 << 20),
        name="backward_own" if which == 0 else "backward_other",
    )(slots, totals, place, values, *parts)


def add(*terms):
    total = terms[0].astype(F32)
    for term in terms[1:]:
        total = total + term.astype(F32)
    return total


def gather_features(mine):
    low, high = send_z(mine, 3), send_z(mine, -3)
    up = send_z(jnp.concatenate([mine, low, high]), 1)
    down = send_z(jnp.concatenate([mine, low]), -1)
    first = jnp.concatenate([mine, low, high, up[0:2]])
    second = jnp.concatenate([up[2:6], down])
    up_first, down_second = send_y(first, 1), send_y(second, -1)
    up_second, down_first = send_y(second, 1), send_y(first, -1)
    far_first, far_second = send_y(up_first, 1), send_y(down_second, -1)
    return [first, second, up_first, down_second, up_second, down_first, far_first, far_second]


def scatter_sum(own, other):
    def here(dy, half, lo=0, hi=8):
        return own[dy * 2 + half, lo:hi], other[dy * 2 + half, lo:hi]

    up_far = send_y(add(*here(2, 0)).astype(BF), 1)
    down_far = send_y(add(*here(2, 1)).astype(BF), -1)
    up_near = send_y(add(*here(1, 1)).astype(BF), 1)
    down_near = send_y(add(*here(3, 0)).astype(BF), -1)
    up_last = send_y(add(*here(1, 0), up_far).astype(BF), 1)
    down_last = send_y(add(*here(3, 1), down_far).astype(BF), -1)

    def first(lo, hi):
        return add(*here(0, 0, lo, hi), down_near[lo:hi], up_last[lo:hi])

    def second(lo, hi):
        return add(*here(0, 1, lo, hi), up_near[lo:hi], down_last[lo:hi])

    up = send_z(first(0, 6).astype(BF), 1)
    down = send_z(second(0, 4).astype(BF), -1)
    high = send_z(add(second(6, 8), up[4:6], down[2:4]).astype(BF), 3)
    low = send_z(add(second(4, 6), up[0:2]).astype(BF), -3)
    return add(first(6, 8), up[2:4], down[0:2], high, low)


def sum_everywhere(terms):
    for step in (1, 2):
        terms = terms + lax.ppermute(terms, "col", [(i, i ^ step) for i in range(NX)])
    for step in (1, 2, 4, 8, 16, 32):
        terms = terms + lax.ppermute(terms, "row", [(i, i ^ step) for i in range(NROW)])
    return terms


def body(features, weight, bias, block_values, block_rows, block_cols, block_counts, cotangent):
    slots = block_values.shape[2]
    values = pltpu.with_memory_space_constraint(block_values[0, 0], pltpu.VMEM)
    place_x = lax.axis_index("col").astype(jnp.int32)
    place_row = lax.axis_index("row").astype(jnp.int32)
    place = place_x.reshape(1)

    gather_table, scatter_table = place_tables()
    columns = block_cols[0, 0]
    chunk = columns // 2
    dz = (chunk // NC - place_row // NC) % NZ
    dy = (chunk // (NC * NZ) - place_row // (NC * NZ)) % NY
    spot = (dy * NZ + dz)[:, None] == jnp.arange(NY * NZ)[None, :]
    gather_at = jnp.sum(jnp.where(spot, gather_table[None, :], 0), axis=1) + columns % 2
    scatter_at = jnp.sum(jnp.where(spot, scatter_table[None, :], 0), axis=1) + columns % 2
    mine = (chunk % NC == place_row % NC).astype(jnp.int32)
    packed = (
        mine
        | (jnp.arange(slots, dtype=jnp.int32) << 1)
        | (block_rows[0, 0] << 10)
        | (gather_at.astype(jnp.int32) << 14)
        | (scatter_at.astype(jnp.int32) << 20)
    )
    own_list, other_list, totals = partition(packed, block_counts.reshape(1))

    pieces = gather_features(features.reshape(2, 128, 128))
    other_pieces = [send_core(piece) for piece in pieces]
    before = forward_own(own_list, totals, values, pieces)
    keep, send1, send2, send3 = forward_other(
        other_list, totals, place, values, other_pieces, before
    )
    got = [send_x(send, step) for step, send in ((1, send1), (2, send2), (3, send3))]
    activated, hidden, terms = layer(keep, got, weight, bias, cotangent)

    parts = [hidden] + [send_x(hidden, step) for step in (1, 2, 3)]
    back_other = backward(1, other_list, totals, place, values, parts)
    from_other = send_core(back_other)
    back_own = backward(0, own_list, totals, place, values, parts)
    split = (8, 8, 128, 128)
    summed = scatter_sum(back_own.reshape(split), from_other.reshape(split))
    feature_grad = jnp.swapaxes(summed, 1, 2).reshape(256, 128)

    scale = 1.0 / math.sqrt(features.shape[0] * NROW * NX)
    terms = sum_everywhere(terms) * scale
    return (activated, feature_grad, terms[0:128], terms[128])


def solution(mesh):
    return jax.shard_map(
        body,
        mesh=mesh,
        in_specs=(
            P(("col", "row"), None),
            P(),
            P(),
            P("row", "col", None, None, None),
            P("row", "col", None),
            P("row", "col", None),
            P("row", "col"),
            P(("row", "col"), None),
        ),
        out_specs=(P(("row", "col"), None), P(("col", "row"), None), P(), P()),
        check_vma=False,
    )
```

```python
import math

import jax
import jax.numpy as jnp
import numpy as np
from jax import lax
from jax.experimental import pallas as pl
from jax.experimental.pallas import tpu as pltpu
from jax.sharding import PartitionSpec as P

BF = jnp.bfloat16
F32 = jnp.float32
I32 = jnp.int32
NY, NZ, NC, NX = 4, 8, 2, 4
NROW = NY * NZ * NC
STEP = 16
LOAD = 16
GATHER_Z = (0, 5, 3, 7, 4, 2, 1, 6)
SCATTER_Z = (6, 1, 4, 0, 7, 2, 5, 3)
GATHER_Y = (0, 3, 1)
SCATTER_Y = (1, 3, 0)
FAR, OTHER, OWN = 0, 1, 2
HIDDEN, TERMS = 256, 144

VMEM = pl.BlockSpec(memory_space=pltpu.VMEM)
SMEM = pl.BlockSpec(memory_space=pltpu.SMEM)
HBM = pl.BlockSpec(memory_space=pltpu.HBM)


def place_table():
    table = np.zeros((2, NY, NZ), np.int32)
    for own in range(2):
        for dy in range(NY):
            for dz in range(NZ):
                gather, scatter = GATHER_Z.index(dz) * 2, SCATTER_Z.index(dz) * 2
                if dy == 2:
                    kind = FAR
                    gather += (1 - own) * 16
                    scatter += (1 - own) * 16
                else:
                    kind = OWN if own else OTHER
                    gather += GATHER_Y.index(dy) * 16 + (1 - own) * 48
                    scatter += SCATTER_Y.index(dy) * 16
                table[own, dy, dz] = kind | (gather << 15) | (scatter << 22)
    return table.reshape(-1)


def slot_of(word):
    return (word >> 2) & 511


def row_of(word):
    return (word >> 11) & 15


def gather_of(word):
    return (word >> 15) & 127


def scatter_of(word):
    return (word >> 22) & 63


def row_moves(dy=0, dz=0):
    moves = []
    for y in range(NY):
        for z in range(NZ):
            for c in range(NC):
                to = (((y + dy) % NY) * NZ + (z + dz) % NZ) * NC + c
                moves.append(((y * NZ + z) * NC + c, to))
    return moves


def send_y(value, step):
    return lax.ppermute(value, "row", row_moves(dy=step))


def send_z(value, step):
    return lax.ppermute(value, "row", row_moves(dz=step))


def swap(value, bit):
    return lax.ppermute(value, "row", [(i, i ^ bit) for i in range(NROW)])


def send_x(value, step):
    return lax.ppermute(value, "col", [(i, (i + step) % NX) for i in range(NX)])


def shape(dims, kind):
    return jax.ShapeDtypeStruct(dims, kind)


def call(kernel, name, outs, args, specs=None, out_specs=None, scratch=(), limit=16):
    single = not isinstance(outs, tuple)
    count = 1 if single else len(outs)
    out_specs = out_specs or [VMEM] * count
    return pl.pallas_call(
        kernel,
        out_shape=outs,
        in_specs=list(specs or [VMEM] * len(args)),
        out_specs=out_specs[0] if single else tuple(out_specs),
        scratch_shapes=list(scratch),
        compiler_params=pltpu.CompilerParams(vmem_limit_bytes=limit << 20),
        cost_estimate=pl.CostEstimate(flops=1, bytes_accessed=1, transcendentals=0),
        name=name,
    )(*args)


def prepare_kernel(rows, columns, count, place, table, values, features, lists, totals, held, mine, sems):
    slots = values.shape[0]
    size = slots + STEP
    filled = count[0, 0]
    me_y, me_z, me_core = place[1], place[2], place[3]

    def load(c):
        part = pl.ds(c * LOAD, LOAD)
        return pltpu.make_async_copy(values.at[part], held.at[part], sems.at[c])

    own_nodes = pltpu.make_async_copy(features, mine, sems.at[slots // LOAD])
    own_nodes.start()
    for c in range(slots // LOAD):
        pl.when(c * LOAD < filled)(lambda c=c: load(c).start())

    def visit(k, found):
        column = columns[0, 0, k]
        own = (((column >> 1) ^ me_core) & 1) ^ 1
        dz = ((column >> 2) - me_z) & (NZ - 1)
        dy = ((column >> 5) - me_y) & (NY - 1)
        entry = table[(own * NY + dy) * NZ + dz]
        kind = entry & 3
        word = entry + (column & 1) * ((1 << 15) + (1 << 22)) + (k << 2) + (rows[0, 0, k] << 11)
        spot = jnp.where(kind == FAR, found[0], jnp.where(kind == OTHER, found[1], found[2]))
        lists[kind * size + spot] = word
        return tuple(n + (kind == i).astype(I32) for i, n in enumerate(found))

    found = lax.fori_loop(0, filled, visit, (0, 0, 0))
    for kind in range(3):
        spare = (8 << 11) | ((32 if kind == FAR else 48) << 22)
        for u in range(STEP):
            lists[kind * size + found[kind] + u] = spare
        totals[kind] = found[kind]
    for c in range(slots // LOAD):
        pl.when(c * LOAD < filled)(lambda c=c: load(c).wait())
    own_nodes.wait()


def in_hbm(value):
    return pltpu.with_memory_space_constraint(value, pltpu.HBM)


def prepare(rows, columns, count, place, values, features):
    slots = values.shape[0]
    return call(
        prepare_kernel,
        "prepare",
        (
            shape((3 * (slots + STEP),), I32),
            shape((3,), I32),
            pltpu.VMEM(values.shape, BF),
            shape(features.shape, BF),
        ),
        (rows, columns, count, place, jnp.asarray(place_table()), in_hbm(values), in_hbm(features)),
        specs=[SMEM] * 5 + [HBM] * 2,
        out_specs=[SMEM, SMEM, VMEM, VMEM],
        scratch=[pltpu.SemaphoreType.DMA((slots // LOAD + 1,))]
    )


def each_slot(kind, lists, totals, size, visit):
    def group(g, carry):
        for u in range(STEP):
            visit(lists[kind * size + g * STEP + u])
        return carry

    lax.fori_loop(0, (totals[kind] + STEP - 1) // STEP, group, 0)


def lay(held, pieces):
    at = 0
    for piece in pieces:
        held[pl.ds(at, piece.shape[0])] = piece[...]
        at += piece.shape[0]


def forward_near_kernel(lists, totals, values, *rest):
    pieces, (out, held, total) = rest[:12], rest[12:]
    size = values.shape[0] + STEP
    lay(held, pieces)
    total[...] = jnp.zeros_like(total)

    def visit(word):
        total[row_of(word)] += jnp.dot(
            values[slot_of(word)], held[gather_of(word)], preferred_element_type=F32
        )

    each_slot(OWN, lists, totals, size, visit)
    each_slot(OTHER, lists, totals, size, visit)
    out[...] = total[0:8]


def forward_far_kernel(lists, totals, place, values, *rest):
    pieces, (before, keep, send1, send2, send3, held, total) = rest[:4], rest[4:]
    size = values.shape[0] + STEP
    lay(held, pieces)
    total[0:8] = before[...]
    total[8] = jnp.zeros_like(total[8])

    def visit(word):
        total[row_of(word)] += jnp.dot(
            values[slot_of(word)], held[gather_of(word)], preferred_element_type=F32
        )

    each_slot(FAR, lists, totals, size, visit)
    x = place[0]
    keep[...] = total[pl.ds(2 * x, 2)]
    for step, send in ((1, send1), (2, send2), (3, send3)):
        send[...] = total[pl.ds(2 * lax.rem(x + step, NX), 2)].astype(BF)


def forward_near(lists, totals, values, pieces):
    return call(
        forward_near_kernel,
        "forward_near",
        shape((8, 128, 128), F32),
        (lists, totals, values, *pieces),
        specs=[SMEM, SMEM] + [VMEM] * 13,
        scratch=[pltpu.VMEM((96, 128, 128), BF), pltpu.VMEM((9, 128, 128), F32)]
    )


def forward_far(lists, totals, place, values, pieces, before):
    part = (2, 128, 128)
    return call(
        forward_far_kernel,
        "forward_far",
        (shape(part, F32), shape(part, BF), shape(part, BF), shape(part, BF)),
        (lists, totals, place, values, *pieces, before),
        specs=[SMEM, SMEM, SMEM] + [VMEM] * 6,
        scratch=[pltpu.VMEM((32, 128, 128), BF), pltpu.VMEM((9, 128, 128), F32)]
    )


def layer_kernel(keep, got1, got2, got3, weight, bias, cotangent, activated, message):
    total = keep[...] + got1[...].astype(F32) + got2[...].astype(F32) + got3[...].astype(F32)
    aggregated = total.reshape(256, 128).astype(BF)
    w = weight[...]
    pre = jnp.dot(aggregated, w, preferred_element_type=F32) + bias[...]
    root = math.sqrt(2.0 / math.pi)
    square = pre * pre
    tanh = jnp.tanh(root * (pre + 0.044715 * (pre * square)))
    cdf = 0.5 * (1.0 + tanh)
    activated[...] = (pre * cdf).astype(BF)
    slope = cdf + 0.5 * pre * (1.0 - tanh * tanh) * (root * (1.0 + 3.0 * 0.044715 * square))
    pre_grad = (cotangent[...].astype(F32) * slope).astype(BF)
    for half in range(2):
        message[half * 128 : half * 128 + 128] = lax.dot_general(
            w, pre_grad[half * 128 : half * 128 + 128], (((1,), (1,)), ((), ())),
            preferred_element_type=F32,
        ).astype(BF)
    message[HIDDEN : HIDDEN + 128] = lax.dot_general(
        aggregated, pre_grad, (((0,), (0,)), ((), ())), preferred_element_type=F32
    ).astype(BF)
    bias_term = jnp.sum(pre_grad.astype(F32), axis=0, keepdims=True)
    message[HIDDEN + 128 : HIDDEN + TERMS] = jnp.broadcast_to(bias_term, (TERMS - 128, 128)).astype(BF)


def layer(keep, got, weight, bias, cotangent):
    return call(
        layer_kernel,
        "layer",
        (shape((256, 128), BF), shape((HIDDEN + TERMS, 128), BF)),
        (keep, *got, weight, bias.reshape(1, 128), cotangent),
    )


def gather_hidden(place, messages, hidden):
    x = place[0]
    for step, part in enumerate(messages):
        at = 2 * lax.rem(x + NX - step, NX)
        hidden[at] = part[0:128]
        hidden[at + 1] = part[128:256]
    hidden[8] = jnp.zeros_like(hidden[8])


def back_products(kind, lists, totals, values, hidden, total):
    total[...] = jnp.zeros_like(total)

    def visit(word):
        total[scatter_of(word)] += jnp.dot(
            hidden[row_of(word)], values[slot_of(word)], preferred_element_type=F32
        )

    each_slot(kind, lists, totals, values.shape[0] + STEP, visit)


def back_far_kernel(lists, totals, place, values, m0, m1, m2, m3, own, other, hidden, total):
    gather_hidden(place, (m0, m1, m2, m3), hidden)
    back_products(FAR, lists, totals, values, hidden, total)
    own[...] = total[0:16].astype(BF)
    other[0:2048] = total[16:32].reshape(2048, 128).astype(BF)
    rows = slice(HIDDEN, HIDDEN + TERMS)
    even = m0[rows].astype(F32) + m2[rows].astype(F32)
    odd = m1[rows].astype(F32) + m3[rows].astype(F32)
    other[2048 : 2048 + TERMS] = (even + odd).astype(BF)


def back_near_kernel(kind, lists, totals, place, values, m0, m1, m2, m3, out, hidden, total):
    gather_hidden(place, (m0, m1, m2, m3), hidden)
    back_products(kind, lists, totals, values, hidden, total)
    out[...] = total[0:48].astype(BF)


def back_far(lists, totals, place, values, messages):
    return call(
        back_far_kernel,
        "back_far",
        (shape((16, 128, 128), BF), shape((2048 + TERMS, 128), BF)),
        (lists, totals, place, values, *messages),
        specs=[SMEM, SMEM, SMEM] + [VMEM] * 5,
        scratch=[pltpu.VMEM((9, 128, 128), BF), pltpu.VMEM((33, 128, 128), F32)]
    )


def back_near(kind, lists, totals, place, values, messages):
    def kernel(*refs):
        back_near_kernel(kind, *refs)

    return call(
        kernel,
        "back_own" if kind == OWN else "back_other",
        shape((48, 128, 128), BF),
        (lists, totals, place, values, *messages),
        specs=[SMEM, SMEM, SMEM] + [VMEM] * 5,
        scratch=[pltpu.VMEM((9, 128, 128), BF), pltpu.VMEM((49, 128, 128), F32)]
    )


def add(*terms):
    total = terms[0].astype(F32)
    for term in terms[1:]:
        total = total + term.astype(F32)
    return total


def sum_far_kernel(own, mine, got, far, terms_out):
    far[...] = add(own[...], got[0:2048].reshape(16, 128, 128)).astype(BF)
    rows = slice(2048, 2048 + TERMS)
    terms_out[...] = add(mine[rows], got[rows])


def sum_near_kernel(own, other, terms, got, up, down, terms_out):
    up[...] = add(own[0:16], other[0:16]).astype(BF)
    down[...] = add(own[16:32], other[16:32]).astype(BF)
    terms_out[...] = terms[...] + got[...]


def sum_here_kernel(own, other, far, from_up, from_down, terms, got, up, down, keep, terms_out):
    first = add(own[32:40], other[32:40], far[0:8], from_up[0:8], from_down[0:8])
    second = add(own[40:48], other[40:48], far[8:16], from_up[8:16], from_down[8:16])
    up[...] = first[0:6].astype(BF)
    down[...] = second[0:4].astype(BF)
    keep[0:2] = first[6:8]
    keep[2:6] = second[4:8]
    terms_out[...] = terms[...] + got[...]


def sum_z_kernel(keep, up, down, terms, got, high, low, here, terms_out):
    low[...] = add(keep[2:4], up[0:2]).astype(BF)
    here[...] = add(keep[0:2], up[2:4], down[0:2])
    high[...] = add(keep[4:6], up[4:6], down[2:4]).astype(BF)
    terms_out[...] = terms[...] + got[...]


def sum_end_kernel(scale, here, high, low, terms, got, feature_grad, weight_grad, bias_grad):
    total = add(here[...], high[...], low[...])
    feature_grad[0:128] = total[0].T
    feature_grad[128:256] = total[1].T
    sums = (terms[...] + got[...]) * scale
    weight_grad[...] = sums[0:128]
    bias_grad[...] = sums[128:136]


def join_kernel(*refs):
    out = refs[-1]
    at = 0
    for ref in refs[:-1]:
        size = min(ref.shape[0], out.shape[0] - at)
        out[pl.ds(at, size)] = ref[0:size]
        at += size


def join(name, size, *parts):
    return call(join_kernel, name, shape((size, 128, 128), BF), parts)


def body(features, weight, bias, block_values, block_rows, block_cols, block_counts, cotangent):
    slots = block_values.shape[2]
    row = lax.axis_index("row").astype(I32)
    place = jnp.stack(
        [lax.axis_index("col").astype(I32), row // (NC * NZ), row // NC % NZ, row % NC]
    )

    nodes = features.reshape(2, 128, 128)
    low, high = send_z(nodes, 3), send_z(nodes, -3)
    lists, totals, values, mine = prepare(
        block_rows, block_cols, block_counts, place, block_values[0, 0], nodes
    )
    values = pltpu.with_memory_space_constraint(values, pltpu.VMEM)
    near = join("join_near", 6, mine, low, high)
    from_up, from_down = send_z(near, 1), send_z(near, -1)
    up_near, down_near = send_y(near, 1), send_y(near, -1)
    other = swap(near, 1)
    from_up, from_down, up_near, down_near, other = lax.optimization_barrier(
        (from_up, from_down, up_near, down_near, other)
    )
    rest = join("join_rest", 10, from_up, from_down)
    up_rest, down_rest = send_y(rest, 1), send_y(rest, -1)
    far_near = send_y(up_near, 1)
    far_rest = send_y(down_rest, -1)
    near_pieces = [near, rest, up_near, up_rest, down_near, down_rest]
    other_near = [other] + [swap(piece, 1) for piece in near_pieces[1:]]
    before = forward_near(lists, totals, values, near_pieces + other_near)
    far_pieces = [far_near, far_rest]
    other_far = [swap(piece, 1) for piece in far_pieces]
    keep, send1, send2, send3 = forward_far(
        lists, totals, place, values, far_pieces + other_far, before
    )

    got = [send_x(send, step) for step, send in ((1, send1), (2, send2), (3, send3))]
    activated, message = layer(keep, got, weight, bias, cotangent)
    messages = [message] + [send_x(message, step) for step in (1, 2, 3)]

    own_far, other_far = back_far(lists, totals, place, values, messages)
    got_far = swap(other_far, 1)
    other_near = back_near(OTHER, lists, totals, place, values, messages)
    other_near, got_far = lax.optimization_barrier((other_near, got_far))
    far, terms = call(
        sum_far_kernel,
        "sum_far",
        (shape((16, 128, 128), BF), shape((TERMS, 128), F32)),
        (own_far, other_far, got_far),
    )
    got_near = swap(other_near, 1)
    got_y_far = send_y(far, 2)
    got_terms = swap(terms, 8)
    own_near = back_near(OWN, lists, totals, place, values, messages)
    terms, got_terms, own_near = lax.optimization_barrier((terms, got_terms, own_near))
    terms = terms + got_terms
    got_terms = swap(terms, 4)
    own_near, got_near, got_y_far = lax.optimization_barrier((own_near, got_near, got_y_far))
    up, down, terms = call(
        sum_near_kernel,
        "sum_near",
        (shape((16, 128, 128), BF),) * 2 + (shape((TERMS, 128), F32),),
        (own_near, got_near, terms, got_terms),
    )
    from_up, from_down = send_y(up, 1), send_y(down, -1)
    got_terms = swap(terms, 2)
    up, down, keep, terms = call(
        sum_here_kernel,
        "sum_here",
        (
            shape((6, 128, 128), BF),
            shape((4, 128, 128), BF),
            shape((6, 128, 128), F32),
            shape((TERMS, 128), F32),
        ),
        (own_near, got_near, got_y_far, from_up, from_down, terms, got_terms),
    )
    up, down = send_z(up, 1), send_z(down, -1)
    got_terms = swap(terms, 16)
    high, low, here, terms = call(
        sum_z_kernel,
        "sum_z",
        (shape((2, 128, 128), BF),) * 2 + (shape((2, 128, 128), F32), shape((TERMS, 128), F32)),
        (keep, up, down, terms, got_terms),
    )
    high, low = send_z(high, 3), send_z(low, -3)
    got_terms = swap(terms, 32)
    scale = 1.0 / math.sqrt(features.shape[0] * NROW * NX)

    def end_kernel(*refs):
        sum_end_kernel(scale, *refs)

    feature_grad, weight_grad, bias_grad = call(
        end_kernel,
        "sum_end",
        (shape((256, 128), F32), shape((128, 128), F32), shape((8, 128), F32)),
        (here, high, low, terms, got_terms),
    )
    return (activated, feature_grad, weight_grad, bias_grad[0])


def solution(mesh):
    return jax.shard_map(
        body,
        mesh=mesh,
        in_specs=(
            P(("col", "row"), None),
            P(),
            P(),
            P("row", "col", None, None, None),
            P("row", "col", None),
            P("row", "col", None),
            P("row", "col"),
            P(("row", "col"), None),
        ),
        out_specs=(P(("row", "col"), None), P(("col", "row"), None), P(), P()),
        check_vma=False,
    )
```

```python
import math

import jax
import jax.numpy as jnp
import numpy as np
from jax import lax
from jax.experimental import pallas as pl
from jax.experimental.pallas import tpu as pltpu
from jax.sharding import PartitionSpec as P

BF = jnp.bfloat16
F32 = jnp.float32
I32 = jnp.int32
NY, NZ, NC, NX = 4, 8, 2, 4
NROW = NY * NZ * NC
STEP = 16
LOAD = 16
GATHER_Z = (0, 5, 3, 7, 4, 2, 1, 6)
SCATTER_Z = (6, 1, 4, 7, 2, 0, 5, 3)
GATHER_Y = (0, 3, 1)
SCATTER_Y = (2, 1, 3, 0)
FAR_OTHER, FAR_OWN, OTHER, OWN = 0, 1, 2, 3
HIDDEN, TERMS = 256, 144

VMEM = pl.BlockSpec(memory_space=pltpu.VMEM)
SMEM = pl.BlockSpec(memory_space=pltpu.SMEM)
HBM = pl.BlockSpec(memory_space=pltpu.HBM)


def place_table():
    table = np.zeros((2, NY, NZ), np.int32)
    for own in range(2):
        for dy in range(NY):
            for dz in range(NZ):
                gather = GATHER_Z.index(dz) * 2
                scatter = SCATTER_Y.index(dy) * 16 + SCATTER_Z.index(dz) * 2
                if dy == 2:
                    kind = FAR_OWN if own else FAR_OTHER
                    gather += (1 - own) * 16
                else:
                    kind = OWN if own else OTHER
                    gather += GATHER_Y.index(dy) * 16 + (1 - own) * 48
                table[own, dy, dz] = kind | (gather << 15) | (scatter << 22)
    return table.reshape(-1)


def slot_of(word):
    return (word >> 2) & 511


def row_of(word):
    return (word >> 11) & 15


def gather_of(word):
    return (word >> 15) & 127


def scatter_of(word):
    return (word >> 22) & 127


def row_moves(dy=0, dz=0):
    moves = []
    for y in range(NY):
        for z in range(NZ):
            for c in range(NC):
                to = (((y + dy) % NY) * NZ + (z + dz) % NZ) * NC + c
                moves.append(((y * NZ + z) * NC + c, to))
    return moves


def send_y(value, step):
    return lax.ppermute(value, "row", row_moves(dy=step))


def send_z(value, step):
    return lax.ppermute(value, "row", row_moves(dz=step))


def swap(value, bit):
    return lax.ppermute(value, "row", [(i, i ^ bit) for i in range(NROW)])


def send_x(value, step):
    return lax.ppermute(value, "col", [(i, (i + step) % NX) for i in range(NX)])


def shape(dims, kind):
    return jax.ShapeDtypeStruct(dims, kind)


def call(kernel, name, outs, args, specs=None, out_specs=None, scratch=(), limit=16):
    single = not isinstance(outs, tuple)
    count = 1 if single else len(outs)
    out_specs = out_specs or [VMEM] * count
    return pl.pallas_call(
        kernel,
        out_shape=outs,
        in_specs=list(specs or [VMEM] * len(args)),
        out_specs=out_specs[0] if single else tuple(out_specs),
        scratch_shapes=list(scratch),
        compiler_params=pltpu.CompilerParams(vmem_limit_bytes=limit << 20),
        cost_estimate=pl.CostEstimate(flops=1, bytes_accessed=1, transcendentals=0),
        name=name,
    )(*args)


def fetch_kernel(features, mine, sem):
    copy = pltpu.make_async_copy(features, mine, sem)
    copy.start()
    copy.wait()


def in_hbm(value):
    return pltpu.with_memory_space_constraint(value, pltpu.HBM)


def fetch(features):
    return call(
        fetch_kernel,
        "fetch",
        shape(features.shape, BF),
        (in_hbm(features),),
        specs=[HBM],
        scratch=[pltpu.SemaphoreType.DMA],
    )


def prepare_kernel(
    rows_in, columns_in, table_in, count, place, values, lists, totals, held, rows, columns, table, sems
):
    slots = values.shape[0]
    size = slots + STEP
    loads = slots // LOAD
    filled = count[0, 0]
    me_y, me_z, me_core = place[1], place[2], place[3]

    def load(c):
        part = pl.ds(c * LOAD, LOAD)
        return pltpu.make_async_copy(values.at[part], held.at[part], sems.at[c])

    small = [
        pltpu.make_async_copy(rows_in, rows, sems.at[loads]),
        pltpu.make_async_copy(columns_in, columns, sems.at[loads + 1]),
        pltpu.make_async_copy(table_in, table, sems.at[loads + 2]),
    ]
    for copy in small:
        copy.start()
    for c in range(loads):
        pl.when(c * LOAD < filled)(lambda c=c: load(c).start())
    for copy in small:
        copy.wait()

    def visit(k, found):
        column = columns[0, 0, k]
        own = (((column >> 1) ^ me_core) & 1) ^ 1
        dz = ((column >> 2) - me_z) & (NZ - 1)
        dy = ((column >> 5) - me_y) & (NY - 1)
        entry = table[(own * NY + dy) * NZ + dz]
        kind = jnp.where(k < filled, entry & 3, 4)
        word = entry + (column & 1) * ((1 << 15) + (1 << 22)) + (k << 2) + (rows[0, 0, k] << 11)
        far = jnp.where(kind == FAR_OTHER, found[0], found[1])
        near = jnp.where(kind == OTHER, found[2], found[3])
        lists[kind * size + jnp.where(kind < OTHER, far, near)] = word
        return tuple(n + (kind == i).astype(I32) for i, n in enumerate(found))

    def group(g, found):
        for u in range(8):
            found = visit(g * 8 + u, found)
        return found

    found = lax.fori_loop(0, (filled + 7) // 8, group, (0, 0, 0, 0))
    spare = (8 << 11) | (64 << 22)
    for kind in range(4):
        for u in range(STEP):
            lists[kind * size + found[kind] + u] = spare
        totals[kind] = found[kind]
    for c in range(loads):
        pl.when(c * LOAD < filled)(lambda c=c: load(c).wait())


def prepare(rows, columns, count, place, values):
    slots = values.shape[0]
    table = jnp.asarray(place_table())
    return call(
        prepare_kernel,
        "prepare",
        (
            shape((5 * (slots + STEP),), I32),
            shape((4,), I32),
            pltpu.VMEM(values.shape, BF),
        ),
        (in_hbm(rows), in_hbm(columns), in_hbm(table), count, place, in_hbm(values)),
        specs=[HBM] * 3 + [SMEM] * 2 + [HBM],
        out_specs=[SMEM, SMEM, VMEM],
        scratch=[
            pltpu.SMEM(rows.shape, I32),
            pltpu.SMEM(columns.shape, I32),
            pltpu.SMEM(table.shape, I32),
            pltpu.SemaphoreType.DMA((slots // LOAD + 3,)),
        ],
    )


def each_slot(kind, lists, totals, size, visit):
    def group(g, carry):
        for u in range(STEP):
            visit(lists[kind * size + g * STEP + u])
        return carry

    lax.fori_loop(0, (totals[kind] + STEP - 1) // STEP, group, 0)


def lay(held, pieces):
    at = 0
    for piece in pieces:
        held[pl.ds(at, piece.shape[0])] = piece[...]
        at += piece.shape[0]


def forward_near_kernel(lists, totals, values, *rest):
    pieces, (out, held, total) = rest[:12], rest[12:]
    size = values.shape[0] + STEP
    lay(held, pieces)
    total[...] = jnp.zeros_like(total)

    def visit(word):
        total[row_of(word)] += jnp.dot(
            values[slot_of(word)], held[gather_of(word)], preferred_element_type=F32
        )

    each_slot(OWN, lists, totals, size, visit)
    each_slot(OTHER, lists, totals, size, visit)
    out[...] = total[0:8]


def forward_far_kernel(lists, totals, place, values, *rest):
    pieces, (before, keep, send1, send2, send3, held, total) = rest[:4], rest[4:]
    size = values.shape[0] + STEP
    lay(held, pieces)
    total[0:8] = before[...]
    total[8] = jnp.zeros_like(total[8])

    def visit(word):
        total[row_of(word)] += jnp.dot(
            values[slot_of(word)], held[gather_of(word)], preferred_element_type=F32
        )

    each_slot(FAR_OWN, lists, totals, size, visit)
    each_slot(FAR_OTHER, lists, totals, size, visit)
    x = place[0]
    keep[...] = total[pl.ds(2 * x, 2)]
    for step, send in ((1, send1), (2, send2), (3, send3)):
        send[...] = total[pl.ds(2 * lax.rem(x + step, NX), 2)].astype(BF)


def forward_near(lists, totals, values, pieces):
    return call(
        forward_near_kernel,
        "forward_near",
        shape((8, 128, 128), F32),
        (lists, totals, values, *pieces),
        specs=[SMEM, SMEM] + [VMEM] * 13,
        scratch=[pltpu.VMEM((96, 128, 128), BF), pltpu.VMEM((9, 128, 128), F32)]
    )


def forward_far(lists, totals, place, values, pieces, before):
    part = (2, 128, 128)
    return call(
        forward_far_kernel,
        "forward_far",
        (shape(part, F32), shape(part, BF), shape(part, BF), shape(part, BF)),
        (lists, totals, place, values, *pieces, before),
        specs=[SMEM, SMEM, SMEM] + [VMEM] * 6,
        scratch=[pltpu.VMEM((32, 128, 128), BF), pltpu.VMEM((9, 128, 128), F32)]
    )


def layer_kernel(keep, got1, got2, got3, weight, bias, cotangent, activated, message):
    total = keep[...] + got1[...].astype(F32) + got2[...].astype(F32) + got3[...].astype(F32)
    aggregated = total.reshape(256, 128).astype(BF)
    w = weight[...]
    pre = jnp.dot(aggregated, w, preferred_element_type=F32) + bias[...]
    root = math.sqrt(2.0 / math.pi)
    square = pre * pre
    tanh = jnp.tanh(root * (pre + 0.044715 * (pre * square)))
    cdf = 0.5 * (1.0 + tanh)
    activated[...] = (pre * cdf).astype(BF)
    slope = cdf + 0.5 * pre * (1.0 - tanh * tanh) * (root * (1.0 + 3.0 * 0.044715 * square))
    pre_grad = (cotangent[...].astype(F32) * slope).astype(BF)
    for half in range(2):
        message[half * 128 : half * 128 + 128] = lax.dot_general(
            w, pre_grad[half * 128 : half * 128 + 128], (((1,), (1,)), ((), ())),
            preferred_element_type=F32,
        ).astype(BF)
    message[HIDDEN : HIDDEN + 128] = lax.dot_general(
        aggregated, pre_grad, (((0,), (0,)), ((), ())), preferred_element_type=F32
    ).astype(BF)
    bias_term = jnp.sum(pre_grad.astype(F32), axis=0, keepdims=True)
    message[HIDDEN + 128 : HIDDEN + TERMS] = jnp.broadcast_to(bias_term, (TERMS - 128, 128)).astype(BF)


def layer(keep, got, weight, bias, cotangent):
    return call(
        layer_kernel,
        "layer",
        (shape((256, 128), BF), shape((HIDDEN + TERMS, 128), BF)),
        (keep, *got, weight, bias.reshape(1, 128), cotangent),
    )


def gather_hidden(place, messages, hidden):
    x = place[0]
    for step, part in enumerate(messages):
        at = 2 * lax.rem(x + NX - step, NX)
        hidden[at] = part[0:128]
        hidden[at + 1] = part[128:256]
    hidden[8] = jnp.zeros_like(hidden[8])


def back_products(kinds, lists, totals, values, hidden, total):
    total[...] = jnp.zeros_like(total)

    def visit(word):
        total[scatter_of(word)] += jnp.dot(
            hidden[row_of(word)], values[slot_of(word)], preferred_element_type=F32
        )

    for kind in kinds:
        each_slot(kind, lists, totals, values.shape[0] + STEP, visit)


def back_other_kernel(lists, totals, place, values, m0, m1, m2, m3, out, hidden, total):
    gather_hidden(place, (m0, m1, m2, m3), hidden)
    back_products((FAR_OTHER, OTHER), lists, totals, values, hidden, total)
    out[0:8192] = total[0:64].reshape(8192, 128).astype(BF)
    rows = slice(HIDDEN, HIDDEN + TERMS)
    even = m0[rows].astype(F32) + m2[rows].astype(F32)
    odd = m1[rows].astype(F32) + m3[rows].astype(F32)
    out[8192 : 8192 + TERMS] = (even + odd).astype(BF)


def back_own_kernel(lists, totals, place, values, m0, m1, m2, m3, out, hidden, total):
    gather_hidden(place, (m0, m1, m2, m3), hidden)
    back_products((FAR_OWN, OWN), lists, totals, values, hidden, total)
    out[...] = total[0:64].astype(BF)


def back(kernel, name, out, lists, totals, place, values, messages):
    return call(
        kernel,
        name,
        out,
        (lists, totals, place, values, *messages),
        specs=[SMEM, SMEM, SMEM] + [VMEM] * 5,
        scratch=[pltpu.VMEM((9, 128, 128), BF), pltpu.VMEM((65, 128, 128), F32)],
    )


def add(*terms):
    total = terms[0].astype(F32)
    for term in terms[1:]:
        total = total + term.astype(F32)
    return total


def sum_core_kernel(own, mine, got, up, down, last, here, terms):
    def both(lo, hi):
        return add(own[lo:hi], got[lo * 128 : hi * 128].reshape(hi - lo, 128, 128))

    up[0:8] = both(0, 8).astype(BF)
    down[0:8] = both(8, 16).astype(BF)
    last[0:8] = both(16, 24)
    up[8:16] = both(24, 32).astype(BF)
    down[8:16] = both(32, 40).astype(BF)
    last[8:16] = both(40, 48)
    here[...] = both(48, 64)
    rows = slice(8192, 8192 + TERMS)
    terms[...] = add(mine[rows], got[rows])


def sum_last_kernel(last, from_up, from_down, up, down):
    up[...] = add(last[0:8], from_up[0:8]).astype(BF)
    down[...] = add(last[8:16], from_down[0:8]).astype(BF)


def sum_y_kernel(here, from_up, from_down, last_up, last_down, up, down, keep):
    first = add(here[0:8], from_down[8:16], last_up[...])
    second = add(here[8:16], from_up[8:16], last_down[...])
    up[...] = first[0:6].astype(BF)
    down[0:2] = first[6:8].astype(BF)
    down[2:4] = second[0:2].astype(BF)
    keep[...] = second[2:8]


def sum_z_kernel(keep, up, down, high, low, here):
    here[...] = add(keep[0:2], up[2:4], down[0:2])
    low[...] = add(keep[2:4], up[0:2]).astype(BF)
    high[...] = add(keep[4:6], up[4:6], down[2:4]).astype(BF)


def sum_end_kernel(scale, here, high, low, terms, feature_grad, weight_grad, bias_grad):
    total = add(here[...], high[...], low[...])
    feature_grad[0:128] = total[0].T
    feature_grad[128:256] = total[1].T
    sums = terms[...] * scale
    weight_grad[...] = sums[0:128]
    bias_grad[...] = sums[128:136]


def join_kernel(*refs):
    out = refs[-1]
    at = 0
    for ref in refs[:-1]:
        size = min(ref.shape[0], out.shape[0] - at)
        out[pl.ds(at, size)] = ref[0:size]
        at += size


def join(name, size, *parts):
    return call(join_kernel, name, shape((size, 128, 128), BF), parts)


def body(features, weight, bias, block_values, block_rows, block_cols, block_counts, cotangent):
    slots = block_values.shape[2]
    row = lax.axis_index("row").astype(I32)
    place = jnp.stack(
        [lax.axis_index("col").astype(I32), row // (NC * NZ), row // NC % NZ, row % NC]
    )

    nodes = features.reshape(2, 128, 128)
    low, high = send_z(nodes, 3), send_z(nodes, -3)
    near = join("join_near", 6, fetch(nodes), low, high)
    from_up, from_down = send_z(near, 1), send_z(near, -1)
    up_near, down_near = send_y(near, 1), send_y(near, -1)
    other_near = swap(near, 1)
    rest = join("join_rest", 10, from_up, from_down)
    rest, up_near, down_near, other_near, place = lax.optimization_barrier(
        (rest, up_near, down_near, other_near, place)
    )
    up_rest, down_rest = send_y(rest, 1), send_y(rest, -1)
    far_near = send_y(up_near, 1)
    lists, totals, values = prepare(
        block_rows, block_cols, block_counts, place, block_values[0, 0]
    )
    values = pltpu.with_memory_space_constraint(values, pltpu.VMEM)
    up_rest, down_rest, lists, totals = lax.optimization_barrier((up_rest, down_rest, lists, totals))
    far_rest = send_y(down_rest, -1)
    near_pieces = [near, rest, up_near, up_rest, down_near, down_rest]
    other_near = [other_near] + [swap(piece, 1) for piece in near_pieces[1:]]
    before = forward_near(lists, totals, values, near_pieces + other_near)
    far_near, far_rest, before = lax.optimization_barrier((far_near, far_rest, before))
    far_pieces = [far_near, far_rest]
    other_far = [swap(piece, 1) for piece in far_pieces]
    keep, send1, send2, send3 = forward_far(
        lists, totals, place, values, far_pieces + other_far, before
    )

    got = [send_x(send, step) for step, send in ((1, send1), (2, send2), (3, send3))]
    activated, message = layer(keep, got, weight, bias, cotangent)
    messages = [message] + [send_x(message, step) for step in (1, 2, 3)]

    back_args = (lists, totals, place, values, messages)
    other = back(back_other_kernel, "back_other", shape((8192 + TERMS, 128), BF), *back_args)
    got = swap(other, 1)
    own = back(back_own_kernel, "back_own", shape((64, 128, 128), BF), *back_args)
    up, down, last, here, terms = call(
        sum_core_kernel,
        "sum_core",
        (
            shape((16, 128, 128), BF),
            shape((16, 128, 128), BF),
            shape((16, 128, 128), F32),
            shape((16, 128, 128), F32),
            shape((TERMS, 128), F32),
        ),
        (own, other, got),
    )
    from_up, from_down = send_y(up, 1), send_y(down, -1)
    for bit in (8, 4):
        terms = terms + swap(terms, bit)
    from_up, from_down, terms = lax.optimization_barrier((from_up, from_down, terms))
    up, down = call(
        sum_last_kernel,
        "sum_last",
        (shape((8, 128, 128), BF),) * 2,
        (last, from_up, from_down),
    )
    last_up, last_down = send_y(up, 1), send_y(down, -1)
    terms = terms + swap(terms, 2)
    last_up, last_down, terms = lax.optimization_barrier((last_up, last_down, terms))
    up, down, keep = call(
        sum_y_kernel,
        "sum_y",
        (shape((6, 128, 128), BF), shape((4, 128, 128), BF), shape((6, 128, 128), F32)),
        (here, from_up, from_down, last_up, last_down),
    )
    up, down = send_z(up, 1), send_z(down, -1)
    terms = terms + swap(terms, 16)
    up, down, terms = lax.optimization_barrier((up, down, terms))
    high, low, here = call(
        sum_z_kernel,
        "sum_z",
        (shape((2, 128, 128), BF),) * 2 + (shape((2, 128, 128), F32),),
        (keep, up, down),
    )
    high, low = send_z(high, 3), send_z(low, -3)
    terms = terms + swap(terms, 32)
    scale = 1.0 / math.sqrt(features.shape[0] * NROW * NX)

    def end_kernel(*refs):
        sum_end_kernel(scale, *refs)

    feature_grad, weight_grad, bias_grad = call(
        end_kernel,
        "sum_end",
        (shape((256, 128), F32), shape((128, 128), F32), shape((8, 128), F32)),
        (here, high, low, terms),
    )
    return (activated, feature_grad, weight_grad, bias_grad[0])


def solution(mesh):
    return jax.shard_map(
        body,
        mesh=mesh,
        in_specs=(
            P(("col", "row"), None),
            P(),
            P(),
            P("row", "col", None, None, None),
            P("row", "col", None),
            P("row", "col", None),
            P("row", "col"),
            P(("row", "col"), None),
        ),
        out_specs=(P(("row", "col"), None), P(("col", "row"), None), P(), P()),
        check_vma=False,
    )
```

```python
import math

import jax
import jax.numpy as jnp
import numpy as np
from jax import lax
from jax.experimental import pallas as pl
from jax.experimental.pallas import tpu as pltpu
from jax.sharding import PartitionSpec as P

BF = jnp.bfloat16
F32 = jnp.float32
I32 = jnp.int32
NY, NZ, NC, NX = 4, 8, 2, 4
NROW = NY * NZ * NC
STEP = 16
LONG = 32
LOAD = 16
GATHER_Z = (0, 5, 3, 7, 4, 2, 1, 6)
SCATTER_Z = (6, 1, 4, 7, 2, 0, 5, 3)
GATHER_Y = (0, 3, 1)
SCATTER_Y = (2, 1, 3, 0)
FAR_OTHER, FAR_OWN, OTHER, OWN = 0, 1, 2, 3
HIDDEN, TERMS = 256, 144
MESSAGES = (0, 1, 3, 2)

VMEM = pl.BlockSpec(memory_space=pltpu.VMEM)
SMEM = pl.BlockSpec(memory_space=pltpu.SMEM)
HBM = pl.BlockSpec(memory_space=pltpu.HBM)


def packed_order(order):
    return sum(order.index(n) << (3 * n) for n in range(max(order) + 1) if n in order)


def describe(rows, columns, place):
    slot = lax.broadcasted_iota(I32, rows.shape, 2)
    own = (((columns >> 1) ^ place[3]) & 1) ^ 1
    dz = ((columns >> 2) - place[2]) & (NZ - 1)
    dy = ((columns >> 5) - place[1]) & (NY - 1)

    def find(order, number):
        return (packed_order(order) >> (3 * number)) & 7

    far = dy == 2
    kind = own + jnp.where(far, 0, 2)
    gather = find(GATHER_Z, dz) * 2 + jnp.where(far, (1 - own) * 16, find(GATHER_Y, dy) * 16 + (1 - own) * 48)
    scatter = find(SCATTER_Z, dz) * 2 + find(SCATTER_Y, dy) * 16
    odd = columns & 1
    return kind | (slot << 2) | (rows << 11) | ((gather + odd) << 15) | ((scatter + odd) << 22)


def slot_of(word):
    return (word >> 2) & 511


def row_of(word):
    return (word >> 11) & 15


def gather_of(word):
    return (word >> 15) & 127


def scatter_of(word):
    return (word >> 22) & 127


def row_moves(dy=0, dz=0):
    moves = []
    for y in range(NY):
        for z in range(NZ):
            for c in range(NC):
                to = (((y + dy) % NY) * NZ + (z + dz) % NZ) * NC + c
                moves.append(((y * NZ + z) * NC + c, to))
    return moves


def send_y(value, step):
    return lax.ppermute(value, "row", row_moves(dy=step))


def send_z(value, step):
    return lax.ppermute(value, "row", row_moves(dz=step))


def swap(value, bit):
    return lax.ppermute(value, "row", [(i, i ^ bit) for i in range(NROW)])


def send_x(value, step):
    return lax.ppermute(value, "col", [(i, (i + step) % NX) for i in range(NX)])


def shape(dims, kind):
    return jax.ShapeDtypeStruct(dims, kind)


def call(kernel, name, outs, args, specs=None, out_specs=None, scratch=(), limit=16):
    single = not isinstance(outs, tuple)
    count = 1 if single else len(outs)
    out_specs = out_specs or [VMEM] * count
    return pl.pallas_call(
        kernel,
        out_shape=outs,
        in_specs=list(specs or [VMEM] * len(args)),
        out_specs=out_specs[0] if single else tuple(out_specs),
        scratch_shapes=list(scratch),
        compiler_params=pltpu.CompilerParams(vmem_limit_bytes=limit << 20),
        cost_estimate=pl.CostEstimate(flops=1, bytes_accessed=1, transcendentals=0),
        name=name,
    )(*args)


def fetch_kernel(features, rows, columns, place, mine, words, sem):
    copy = pltpu.make_async_copy(features, mine, sem)
    copy.start()
    words[...] = describe(rows[...], columns[...], place)
    copy.wait()


def in_hbm(value):
    return pltpu.with_memory_space_constraint(value, pltpu.HBM)


def fetch(features, rows, columns, place):
    return call(
        fetch_kernel,
        "fetch",
        (shape(features.shape, BF), shape(rows.shape, I32)),
        (in_hbm(features), rows, columns, place),
        specs=[HBM, VMEM, VMEM, SMEM],
        scratch=[pltpu.SemaphoreType.DMA],
    )


def prepare_kernel(words_in, count, values, lists, totals, held, words, sems):
    slots = values.shape[0]
    size = slots + STEP
    loads = slots // LOAD
    filled = count[0, 0]

    def load(c):
        part = pl.ds(c * LOAD, LOAD)
        return pltpu.make_async_copy(values.at[part], held.at[part], sems.at[c])

    all_words = pltpu.make_async_copy(words_in, words, sems.at[loads])
    all_words.start()
    for c in range(loads):
        pl.when(c * LOAD < filled)(lambda c=c: load(c).start())
    all_words.wait()

    def visit(k, found):
        word = words[0, 0, k]
        kind = jnp.where(k < filled, word & 3, 4)
        far = jnp.where(kind == FAR_OTHER, found[0], found[1])
        near = jnp.where(kind == OTHER, found[2], found[3])
        lists[kind * size + jnp.where(kind < OTHER, far, near)] = word
        return tuple(n + (kind == i).astype(I32) for i, n in enumerate(found))

    def group(g, found):
        for u in range(8):
            found = visit(g * 8 + u, found)
        return found

    found = lax.fori_loop(0, (filled + 7) // 8, group, (0, 0, 0, 0))
    spare = (8 << 11) | (64 << 22)
    for kind in range(4):
        for u in range(STEP):
            lists[kind * size + found[kind] + u] = spare
        totals[kind] = found[kind]
    for c in range(loads):
        pl.when(c * LOAD < filled)(lambda c=c: load(c).wait())


def prepare(words, count, values):
    slots = values.shape[0]
    return call(
        prepare_kernel,
        "prepare",
        (
            shape((5 * (slots + STEP),), I32),
            shape((4,), I32),
            pltpu.VMEM(values.shape, BF),
        ),
        (words, count, in_hbm(values)),
        specs=[VMEM, SMEM, HBM],
        out_specs=[SMEM, SMEM, VMEM],
        scratch=[pltpu.SMEM(words.shape, I32), pltpu.SemaphoreType.DMA((slots // LOAD + 1,))],
    )


def each_slot(kind, lists, totals, size, visit):
    def group(start, length):
        def step(g, carry):
            for u in range(length):
                visit(lists[kind * size + start + g * length + u])
            return carry

        return step

    count = totals[kind]
    long = count // LONG
    lax.fori_loop(0, long, group(0, LONG), 0)
    lax.fori_loop(0, (count - long * LONG + STEP - 1) // STEP, group(long * LONG, STEP), 0)


def lay(held, pieces):
    at = 0
    for piece in pieces:
        held[pl.ds(at, piece.shape[0])] = piece[...]
        at += piece.shape[0]


def forward_near_kernel(lists, totals, values, *rest):
    pieces, (out, held, total) = rest[:12], rest[12:]
    size = values.shape[0] + STEP
    lay(held, pieces)
    total[...] = jnp.zeros_like(total)

    def visit(word):
        total[row_of(word)] += jnp.dot(
            values[slot_of(word)], held[gather_of(word)], preferred_element_type=F32
        )

    each_slot(OWN, lists, totals, size, visit)
    each_slot(OTHER, lists, totals, size, visit)
    out[...] = total[0:8]


def forward_far_kernel(lists, totals, place, values, *rest):
    pieces, (before, keep, send1, send2, send3, held, total) = rest[:4], rest[4:]
    size = values.shape[0] + STEP
    lay(held, pieces)
    total[0:8] = before[...]
    total[8] = jnp.zeros_like(total[8])

    def visit(word):
        total[row_of(word)] += jnp.dot(
            values[slot_of(word)], held[gather_of(word)], preferred_element_type=F32
        )

    each_slot(FAR_OWN, lists, totals, size, visit)
    each_slot(FAR_OTHER, lists, totals, size, visit)
    x = place[0]
    keep[...] = total[pl.ds(2 * x, 2)]
    for step, send in ((1, send1), (2, send2), (3, send3)):
        send[...] = total[pl.ds(2 * lax.rem(x + step, NX), 2)].astype(BF)


def forward_near(lists, totals, values, pieces):
    return call(
        forward_near_kernel,
        "forward_near",
        shape((8, 128, 128), F32),
        (lists, totals, values, *pieces),
        specs=[SMEM, SMEM] + [VMEM] * 13,
        scratch=[pltpu.VMEM((96, 128, 128), BF), pltpu.VMEM((9, 128, 128), F32)]
    )


def forward_far(lists, totals, place, values, pieces, before):
    part = (2, 128, 128)
    return call(
        forward_far_kernel,
        "forward_far",
        (shape(part, F32), shape(part, BF), shape(part, BF), shape(part, BF)),
        (lists, totals, place, values, *pieces, before),
        specs=[SMEM, SMEM, SMEM] + [VMEM] * 6,
        scratch=[pltpu.VMEM((32, 128, 128), BF), pltpu.VMEM((9, 128, 128), F32)]
    )


def layer_kernel(keep, got1, got2, got3, weight, bias, cotangent, activated, message):
    total = keep[...] + got1[...].astype(F32) + got2[...].astype(F32) + got3[...].astype(F32)
    aggregated = total.reshape(256, 128).astype(BF)
    w = weight[...]
    pre = jnp.dot(aggregated, w, preferred_element_type=F32) + bias[...]
    root = math.sqrt(2.0 / math.pi)
    square = pre * pre
    tanh = jnp.tanh(root * (pre + 0.044715 * (pre * square)))
    cdf = 0.5 * (1.0 + tanh)
    activated[...] = (pre * cdf).astype(BF)
    slope = cdf + 0.5 * pre * (1.0 - tanh * tanh) * (root * (1.0 + 3.0 * 0.044715 * square))
    pre_grad = (cotangent[...].astype(F32) * slope).astype(BF)
    for half in range(2):
        message[half * 128 : half * 128 + 128] = lax.dot_general(
            w, pre_grad[half * 128 : half * 128 + 128], (((1,), (1,)), ((), ())),
            preferred_element_type=F32,
        ).astype(BF)
    message[HIDDEN : HIDDEN + 128] = lax.dot_general(
        aggregated, pre_grad, (((0,), (0,)), ((), ())), preferred_element_type=F32
    ).astype(BF)
    bias_term = jnp.sum(pre_grad.astype(F32), axis=0, keepdims=True)
    message[HIDDEN + 128 : HIDDEN + TERMS] = jnp.broadcast_to(bias_term, (TERMS - 128, 128)).astype(BF)


def layer(keep, got, weight, bias, cotangent):
    return call(
        layer_kernel,
        "layer",
        (shape((256, 128), BF), shape((HIDDEN + TERMS, 128), BF)),
        (keep, *got, weight, bias.reshape(1, 128), cotangent),
    )


def gather_hidden(place, messages, hidden):
    x = place[0]
    for step, part in zip(MESSAGES, messages):
        at = 2 * lax.rem(x + NX - step, NX)
        hidden[at] = part[0:128]
        hidden[at + 1] = part[128:256]
    hidden[8] = jnp.zeros_like(hidden[8])


def back_products(kinds, lists, totals, values, hidden, total):
    total[...] = jnp.zeros_like(total)

    def visit(word):
        total[scatter_of(word)] += jnp.dot(
            hidden[row_of(word)], values[slot_of(word)], preferred_element_type=F32
        )

    for kind in kinds:
        each_slot(kind, lists, totals, values.shape[0] + STEP, visit)


def back_other_kernel(lists, totals, place, values, m0, m1, m2, m3, out, hidden, total):
    gather_hidden(place, (m0, m1, m2, m3), hidden)
    back_products((FAR_OTHER, OTHER), lists, totals, values, hidden, total)
    out[0:8192] = total[0:64].reshape(8192, 128).astype(BF)
    rows = slice(HIDDEN, HIDDEN + TERMS)
    even = m0[rows].astype(F32) + m3[rows].astype(F32)
    odd = m1[rows].astype(F32) + m2[rows].astype(F32)
    out[8192 : 8192 + TERMS] = (even + odd).astype(BF)


def back_own_kernel(lists, totals, place, values, m0, m1, m2, m3, out, hidden, total):
    gather_hidden(place, (m0, m1, m2, m3), hidden)
    back_products((FAR_OWN, OWN), lists, totals, values, hidden, total)
    out[...] = total[0:64].astype(BF)


def back(kernel, name, out, lists, totals, place, values, messages):
    return call(
        kernel,
        name,
        out,
        (lists, totals, place, values, *messages),
        specs=[SMEM, SMEM, SMEM] + [VMEM] * 5,
        scratch=[pltpu.VMEM((9, 128, 128), BF), pltpu.VMEM((65, 128, 128), F32)],
    )


def add(*terms):
    total = terms[0].astype(F32)
    for term in terms[1:]:
        total = total + term.astype(F32)
    return total


def sum_core_kernel(own, mine, got, up, down, last, here, terms):
    def both(lo, hi):
        return add(own[lo:hi], got[lo * 128 : hi * 128].reshape(hi - lo, 128, 128))

    up[0:8] = both(0, 8).astype(BF)
    down[0:8] = both(8, 16).astype(BF)
    last[0:8] = both(16, 24)
    up[8:16] = both(24, 32).astype(BF)
    down[8:16] = both(32, 40).astype(BF)
    last[8:16] = both(40, 48)
    here[...] = both(48, 64)
    rows = slice(8192, 8192 + TERMS)
    terms[...] = add(mine[rows], got[rows])


def sum_last_kernel(last, from_up, from_down, up, down):
    up[...] = add(last[0:8], from_up[0:8]).astype(BF)
    down[...] = add(last[8:16], from_down[0:8]).astype(BF)


def sum_y_kernel(here, from_up, from_down, last_up, last_down, up, down, keep):
    first = add(here[0:8], from_down[8:16], last_up[...])
    second = add(here[8:16], from_up[8:16], last_down[...])
    up[...] = first[0:6].astype(BF)
    down[0:2] = first[6:8].astype(BF)
    down[2:4] = second[0:2].astype(BF)
    keep[...] = second[2:8]


def sum_z_kernel(keep, up, down, terms, high, low, here, short):
    here[...] = add(keep[0:2], up[2:4], down[0:2])
    low[...] = add(keep[2:4], up[0:2]).astype(BF)
    high[...] = add(keep[4:6], up[4:6], down[2:4]).astype(BF)
    short[...] = terms[...].astype(BF)


def sum_end_kernel(scale, here, high, low, short, got, feature_grad, weight_grad, bias_grad):
    total = add(here[...], high[...], low[...])
    feature_grad[0:128] = total[0].T
    feature_grad[128:256] = total[1].T
    sums = add(short[...], got[...]) * scale
    weight_grad[...] = sums[0:128]
    bias_grad[...] = sums[128:129]


def join_kernel(*refs):
    out = refs[-1]
    at = 0
    for ref in refs[:-1]:
        size = min(ref.shape[0], out.shape[0] - at)
        out[pl.ds(at, size)] = ref[0:size]
        at += size


def join(name, size, *parts):
    return call(join_kernel, name, shape((size, 128, 128), BF), parts)


def body(features, weight, bias, block_values, block_rows, block_cols, block_counts, cotangent):
    slots = block_values.shape[2]
    row = lax.axis_index("row").astype(I32)
    place = jnp.stack(
        [lax.axis_index("col").astype(I32), row // (NC * NZ), row // NC % NZ, row % NC]
    )

    nodes = features.reshape(2, 128, 128)
    low, high = send_z(nodes, 3), send_z(nodes, -3)
    mine, words = fetch(nodes, block_rows, block_cols, place)
    near = join("join_near", 6, mine, low, high)
    from_up, from_down = send_z(near, 1), send_z(near, -1)
    up_near, down_near = send_y(near, 1), send_y(near, -1)
    other_near = swap(near, 1)
    rest = join("join_rest", 10, from_up, from_down)
    rest, up_near, down_near, other_near, words = lax.optimization_barrier(
        (rest, up_near, down_near, other_near, words)
    )
    up_rest, down_rest = send_y(rest, 1), send_y(rest, -1)
    far_near = send_y(up_near, 1)
    lists, totals, values = prepare(words, block_counts, block_values[0, 0])
    values = pltpu.with_memory_space_constraint(values, pltpu.VMEM)
    up_rest, down_rest, lists, totals = lax.optimization_barrier((up_rest, down_rest, lists, totals))
    far_rest = send_y(down_rest, -1)
    near_pieces = [near, rest, up_near, up_rest, down_near, down_rest]
    other_near = [other_near] + [swap(piece, 1) for piece in near_pieces[1:]]
    before = forward_near(lists, totals, values, near_pieces + other_near)
    far_near, far_rest, before = lax.optimization_barrier((far_near, far_rest, before))
    far_pieces = [far_near, far_rest]
    other_far = [swap(piece, 1) for piece in far_pieces]
    keep, send1, send2, send3 = forward_far(
        lists, totals, place, values, far_pieces + other_far, before
    )

    got = [send_x(send, step) for step, send in ((2, send2), (1, send1), (3, send3))]
    activated, message = layer(keep, got, weight, bias, cotangent)
    messages = [message] + [send_x(message, step) for step in MESSAGES[1:]]

    back_args = (lists, totals, place, values, messages)
    other = back(back_other_kernel, "back_other", shape((8192 + TERMS, 128), BF), *back_args)
    got = swap(other, 1)
    own = back(back_own_kernel, "back_own", shape((64, 128, 128), BF), *back_args)
    up, down, last, here, terms = call(
        sum_core_kernel,
        "sum_core",
        (
            shape((16, 128, 128), BF),
            shape((16, 128, 128), BF),
            shape((16, 128, 128), F32),
            shape((16, 128, 128), F32),
            shape((TERMS, 128), F32),
        ),
        (own, other, got),
    )
    from_up, from_down = send_y(up, 1), send_y(down, -1)
    for bit in (8, 4):
        terms = terms + swap(terms, bit)
    from_up, from_down, terms = lax.optimization_barrier((from_up, from_down, terms))
    up, down = call(
        sum_last_kernel,
        "sum_last",
        (shape((8, 128, 128), BF),) * 2,
        (last, from_up, from_down),
    )
    last_up, last_down = send_y(up, 1), send_y(down, -1)
    terms = terms + swap(terms, 2)
    last_up, last_down, terms = lax.optimization_barrier((last_up, last_down, terms))
    up, down, keep = call(
        sum_y_kernel,
        "sum_y",
        (shape((6, 128, 128), BF), shape((4, 128, 128), BF), shape((6, 128, 128), F32)),
        (here, from_up, from_down, last_up, last_down),
    )
    up, down = send_z(up, 1), send_z(down, -1)
    terms = terms + swap(terms, 16)
    up, down, terms = lax.optimization_barrier((up, down, terms))
    high, low, here, short = call(
        sum_z_kernel,
        "sum_z",
        (shape((2, 128, 128), BF),) * 2 + (shape((2, 128, 128), F32), shape((TERMS, 128), BF)),
        (keep, up, down, terms),
    )
    high, low = send_z(high, 3), send_z(low, -3)
    got_short = swap(short, 32)
    scale = 1.0 / math.sqrt(features.shape[0] * NROW * NX)

    def end_kernel(*refs):
        sum_end_kernel(scale, *refs)

    feature_grad, weight_grad, bias_grad = call(
        end_kernel,
        "sum_end",
        (shape((256, 128), F32), shape((128, 128), F32), shape((1, 128), F32)),
        (here, high, low, short, got_short),
    )
    return (activated, feature_grad, weight_grad, bias_grad.reshape(128))


def solution(mesh):
    return jax.shard_map(
        body,
        mesh=mesh,
        in_specs=(
            P(("col", "row"), None),
            P(),
            P(),
            P("row", "col", None, None, None),
            P("row", "col", None),
            P("row", "col", None),
            P("row", "col"),
            P(("row", "col"), None),
        ),
        out_specs=(P(("row", "col"), None), P(("col", "row"), None), P(), P()),
        check_vma=False,
    )
```

```python
import math

import jax
import jax.numpy as jnp
import numpy as np
from jax import lax
from jax.experimental import pallas as pl
from jax.experimental.pallas import tpu as pltpu
from jax.sharding import PartitionSpec as P

BF = jnp.bfloat16
F32 = jnp.float32
I32 = jnp.int32
NY, NZ, NC, NX = 4, 8, 2, 4
NROW = NY * NZ * NC
STEP = 16
LONG = 32
LOAD = 16
GATHER_Z = (0, 5, 3, 7, 4, 2, 1, 6)
SCATTER_Z = (6, 1, 4, 7, 2, 0, 5, 3)
GATHER_Y = (0, 3, 1)
SCATTER_Y = (2, 1, 3, 0)
FAR_OTHER, FAR_OWN, OTHER, OWN = 0, 1, 2, 3
HIDDEN, TERMS = 256, 144
MESSAGES = (0, 1, 3, 2)

VMEM = pl.BlockSpec(memory_space=pltpu.VMEM)
SMEM = pl.BlockSpec(memory_space=pltpu.SMEM)
HBM = pl.BlockSpec(memory_space=pltpu.HBM)


def packed_order(order):
    return sum(order.index(n) << (3 * n) for n in range(max(order) + 1) if n in order)


def describe(rows, columns, place):
    slot = lax.broadcasted_iota(I32, rows.shape, 2)
    own = (((columns >> 1) ^ place[3]) & 1) ^ 1
    dz = ((columns >> 2) - place[2]) & (NZ - 1)
    dy = ((columns >> 5) - place[1]) & (NY - 1)

    def find(order, number):
        return (packed_order(order) >> (3 * number)) & 7

    far = dy == 2
    kind = own + jnp.where(far, 0, 2)
    gather = find(GATHER_Z, dz) * 2 + jnp.where(far, (1 - own) * 16, find(GATHER_Y, dy) * 16 + (1 - own) * 48)
    scatter = find(SCATTER_Z, dz) * 2 + find(SCATTER_Y, dy) * 16
    odd = columns & 1
    return kind | (slot << 2) | (rows << 11) | ((gather + odd) << 15) | ((scatter + odd) << 22)


def slot_of(word):
    return (word >> 2) & 511


def row_of(word):
    return (word >> 11) & 15


def gather_of(word):
    return (word >> 15) & 127


def scatter_of(word):
    return (word >> 22) & 127


def row_moves(dy=0, dz=0):
    moves = []
    for y in range(NY):
        for z in range(NZ):
            for c in range(NC):
                to = (((y + dy) % NY) * NZ + (z + dz) % NZ) * NC + c
                moves.append(((y * NZ + z) * NC + c, to))
    return moves


def send_y(value, step):
    return lax.ppermute(value, "row", row_moves(dy=step))


def send_z(value, step):
    return lax.ppermute(value, "row", row_moves(dz=step))


def swap(value, bit):
    return lax.ppermute(value, "row", [(i, i ^ bit) for i in range(NROW)])


def send_x(value, step):
    return lax.ppermute(value, "col", [(i, (i + step) % NX) for i in range(NX)])


def shape(dims, kind):
    return jax.ShapeDtypeStruct(dims, kind)


def call(kernel, name, outs, args, specs=None, out_specs=None, scratch=(), limit=16):
    single = not isinstance(outs, tuple)
    count = 1 if single else len(outs)
    out_specs = out_specs or [VMEM] * count
    return pl.pallas_call(
        kernel,
        out_shape=outs,
        in_specs=list(specs or [VMEM] * len(args)),
        out_specs=out_specs[0] if single else tuple(out_specs),
        scratch_shapes=list(scratch),
        compiler_params=pltpu.CompilerParams(vmem_limit_bytes=limit << 20),
        cost_estimate=pl.CostEstimate(flops=1, bytes_accessed=1, transcendentals=0),
        name=name,
    )(*args)


def fetch_kernel(features, rows, columns, place, mine, words, sem):
    copy = pltpu.make_async_copy(features, mine, sem)
    copy.start()
    words[...] = describe(rows[...], columns[...], place)
    copy.wait()


def in_hbm(value):
    return pltpu.with_memory_space_constraint(value, pltpu.HBM)


def fetch(features, rows, columns, place):
    return call(
        fetch_kernel,
        "fetch",
        (shape(features.shape, BF), shape(rows.shape, I32)),
        (in_hbm(features), rows, columns, place),
        specs=[HBM, VMEM, VMEM, SMEM],
        scratch=[pltpu.SemaphoreType.DMA],
    )


def prepare_kernel(words_in, count, values, lists, totals, held, words, sems):
    slots = values.shape[0]
    size = slots + STEP
    loads = slots // LOAD
    filled = count[0, 0]

    def load(c):
        part = pl.ds(c * LOAD, LOAD)
        return pltpu.make_async_copy(values.at[part], held.at[part], sems.at[c])

    all_words = pltpu.make_async_copy(words_in, words, sems.at[loads])
    all_words.start()
    for c in range(loads):
        pl.when(c * LOAD < filled)(lambda c=c: load(c).start())
    all_words.wait()

    def visit(k, found):
        word = words[0, 0, k]
        kind = jnp.where(k < filled, word & 3, 4)
        far = jnp.where(kind == FAR_OTHER, found[0], found[1])
        near = jnp.where(kind == OTHER, found[2], found[3])
        lists[kind * size + jnp.where(kind < OTHER, far, near)] = word
        return tuple(n + (kind == i).astype(I32) for i, n in enumerate(found))

    def group(g, found):
        for u in range(8):
            found = visit(g * 8 + u, found)
        return found

    found = lax.fori_loop(0, (filled + 7) // 8, group, (0, 0, 0, 0))
    spare = (8 << 11) | (64 << 22)
    for kind in range(4):
        for u in range(STEP):
            lists[kind * size + found[kind] + u] = spare
        totals[kind] = found[kind]
    for c in range(loads):
        pl.when(c * LOAD < filled)(lambda c=c: load(c).wait())


def prepare(words, count, values):
    slots = values.shape[0]
    return call(
        prepare_kernel,
        "prepare",
        (
            shape((5 * (slots + STEP),), I32),
            shape((4,), I32),
            pltpu.VMEM(values.shape, BF),
        ),
        (words, count, in_hbm(values)),
        specs=[VMEM, SMEM, HBM],
        out_specs=[SMEM, SMEM, VMEM],
        scratch=[pltpu.SMEM(words.shape, I32), pltpu.SemaphoreType.DMA((slots // LOAD + 1,))],
    )


def each_slot(kind, lists, totals, size, visit):
    def group(start, length):
        def step(g, carry):
            for u in range(length):
                visit(lists[kind * size + start + g * length + u])
            return carry

        return step

    count = totals[kind]
    long = count // LONG
    lax.fori_loop(0, long, group(0, LONG), 0)
    lax.fori_loop(0, (count - long * LONG + STEP - 1) // STEP, group(long * LONG, STEP), 0)


def lay(held, pieces):
    at = 0
    for piece in pieces:
        held[pl.ds(at, piece.shape[0])] = piece[...]
        at += piece.shape[0]


def forward_near_kernel(lists, totals, values, *rest):
    pieces, (out, held, total) = rest[:12], rest[12:]
    size = values.shape[0] + STEP
    lay(held, pieces)
    total[...] = jnp.zeros_like(total)

    def visit(word):
        total[row_of(word)] += jnp.dot(
            values[slot_of(word)], held[gather_of(word)], preferred_element_type=F32
        )

    each_slot(OWN, lists, totals, size, visit)
    each_slot(OTHER, lists, totals, size, visit)
    out[...] = total[0:8]


def forward_far_kernel(lists, totals, place, values, *rest):
    pieces, (before, keep, send1, send2, send3, held, total) = rest[:4], rest[4:]
    size = values.shape[0] + STEP
    lay(held, pieces)
    total[0:8] = before[...]
    total[8] = jnp.zeros_like(total[8])

    def visit(word):
        total[row_of(word)] += jnp.dot(
            values[slot_of(word)], held[gather_of(word)], preferred_element_type=F32
        )

    each_slot(FAR_OWN, lists, totals, size, visit)
    each_slot(FAR_OTHER, lists, totals, size, visit)
    x = place[0]
    keep[...] = total[pl.ds(2 * x, 2)]
    for step, send in ((1, send1), (2, send2), (3, send3)):
        send[...] = total[pl.ds(2 * lax.rem(x + step, NX), 2)].astype(BF)


def forward_near(lists, totals, values, pieces):
    return call(
        forward_near_kernel,
        "forward_near",
        shape((8, 128, 128), F32),
        (lists, totals, values, *pieces),
        specs=[SMEM, SMEM] + [VMEM] * 13,
        scratch=[pltpu.VMEM((96, 128, 128), BF), pltpu.VMEM((9, 128, 128), F32)]
    )


def forward_far(lists, totals, place, values, pieces, before):
    part = (2, 128, 128)
    return call(
        forward_far_kernel,
        "forward_far",
        (shape(part, F32), shape(part, BF), shape(part, BF), shape(part, BF)),
        (lists, totals, place, values, *pieces, before),
        specs=[SMEM, SMEM, SMEM] + [VMEM] * 6,
        scratch=[pltpu.VMEM((32, 128, 128), BF), pltpu.VMEM((9, 128, 128), F32)]
    )


def layer_kernel(keep, got1, got2, got3, weight, bias, cotangent, activated, message):
    total = keep[...] + got1[...].astype(F32) + got2[...].astype(F32) + got3[...].astype(F32)
    aggregated = total.reshape(256, 128).astype(BF)
    w = weight[...]
    pre = jnp.dot(aggregated, w, preferred_element_type=F32) + bias[...]
    root = math.sqrt(2.0 / math.pi)
    square = pre * pre
    tanh = jnp.tanh(root * (pre + 0.044715 * (pre * square)))
    cdf = 0.5 * (1.0 + tanh)
    activated[...] = (pre * cdf).astype(BF)
    slope = cdf + 0.5 * pre * (1.0 - tanh * tanh) * (root * (1.0 + 3.0 * 0.044715 * square))
    pre_grad = (cotangent[...].astype(F32) * slope).astype(BF)
    for half in range(2):
        message[half * 128 : half * 128 + 128] = lax.dot_general(
            w, pre_grad[half * 128 : half * 128 + 128], (((1,), (1,)), ((), ())),
            preferred_element_type=F32,
        ).astype(BF)
    message[HIDDEN : HIDDEN + 128] = lax.dot_general(
        aggregated, pre_grad, (((0,), (0,)), ((), ())), preferred_element_type=F32
    ).astype(BF)
    bias_term = jnp.sum(pre_grad.astype(F32), axis=0, keepdims=True)
    message[HIDDEN + 128 : HIDDEN + TERMS] = jnp.broadcast_to(bias_term, (TERMS - 128, 128)).astype(BF)


def layer(keep, got, weight, bias, cotangent):
    return call(
        layer_kernel,
        "layer",
        (shape((256, 128), BF), shape((HIDDEN + TERMS, 128), BF)),
        (keep, *got, weight, bias.reshape(1, 128), cotangent),
    )


def gather_hidden(place, messages, hidden):
    x = place[0]
    for step, part in zip(MESSAGES, messages):
        at = 2 * lax.rem(x + NX - step, NX)
        hidden[at] = part[0:128]
        hidden[at + 1] = part[128:256]
    hidden[8] = jnp.zeros_like(hidden[8])


def back_products(kinds, lists, totals, values, hidden, total):
    total[...] = jnp.zeros_like(total)

    def visit(word):
        total[scatter_of(word)] += jnp.dot(
            hidden[row_of(word)], values[slot_of(word)], preferred_element_type=F32
        )

    for kind in kinds:
        each_slot(kind, lists, totals, values.shape[0] + STEP, visit)


def back_other_kernel(lists, totals, place, values, m0, m1, m2, m3, out, hidden, total):
    gather_hidden(place, (m0, m1, m2, m3), hidden)
    back_products((FAR_OTHER, OTHER), lists, totals, values, hidden, total)
    out[0:8192] = total[0:64].reshape(8192, 128).astype(BF)
    rows = slice(HIDDEN, HIDDEN + TERMS)
    even = m0[rows].astype(F32) + m3[rows].astype(F32)
    odd = m1[rows].astype(F32) + m2[rows].astype(F32)
    out[8192 : 8192 + TERMS] = (even + odd).astype(BF)


def back_own_kernel(lists, totals, place, values, m0, m1, m2, m3, out, hidden, total):
    gather_hidden(place, (m0, m1, m2, m3), hidden)
    back_products((FAR_OWN, OWN), lists, totals, values, hidden, total)
    out[...] = total[0:64].astype(BF)


def back(kernel, name, out, lists, totals, place, values, messages):
    return call(
        kernel,
        name,
        out,
        (lists, totals, place, values, *messages),
        specs=[SMEM, SMEM, SMEM] + [VMEM] * 5,
        scratch=[pltpu.VMEM((9, 128, 128), BF), pltpu.VMEM((65, 128, 128), F32)],
    )


def add(*terms):
    total = terms[0].astype(F32)
    for term in terms[1:]:
        total = total + term.astype(F32)
    return total


def sum_core_kernel(own, mine, got, up, down, last, here, terms):
    def both(lo, hi):
        return add(own[lo:hi], got[lo * 128 : hi * 128].reshape(hi - lo, 128, 128))

    up[0:8] = both(0, 8).astype(BF)
    down[0:8] = both(8, 16).astype(BF)
    last[0:8] = both(16, 24)
    up[8:16] = both(24, 32).astype(BF)
    down[8:16] = both(32, 40).astype(BF)
    last[8:16] = both(40, 48)
    here[...] = both(48, 64)
    rows = slice(8192, 8192 + TERMS)
    terms[...] = add(mine[rows], got[rows])


def sum_last_kernel(last, from_up, from_down, terms, up, down, short):
    up[0:1024] = add(last[0:8], from_up[0:8]).reshape(1024, 128).astype(BF)
    down[0:1024] = add(last[8:16], from_down[0:8]).reshape(1024, 128).astype(BF)
    short[...] = terms[...].astype(BF)
    for message in (up, down):
        message[1024 : 1024 + TERMS] = terms[...].astype(BF)


def sum_y_kernel(here, from_up, from_down, last_up, last_down, short, got, up, down, keep, terms):
    first = add(here[0:8], from_down[8:16], last_up[0:1024].reshape(8, 128, 128))
    second = add(here[8:16], from_up[8:16], last_down[0:1024].reshape(8, 128, 128))
    up[...] = first[0:6].astype(BF)
    down[0:2] = first[6:8].astype(BF)
    down[2:4] = second[0:2].astype(BF)
    keep[...] = second[2:8]
    rows = slice(1024, 1024 + TERMS)
    terms[...] = add(short[...], got[...]) + add(last_up[rows], last_down[rows])


def sum_z_kernel(keep, up, down, high, low, here):
    here[...] = add(keep[0:2], up[2:4], down[0:2])
    low[...] = add(keep[2:4], up[0:2]).astype(BF)
    high[...] = add(keep[4:6], up[4:6], down[2:4]).astype(BF)


def sum_end_kernel(scale, here, high, low, terms, got, feature_grad, weight_grad, bias_grad):
    total = add(here[...], high[...], low[...])
    feature_grad[0:128] = total[0].T
    feature_grad[128:256] = total[1].T
    sums = (terms[...] + got[...]) * scale
    weight_grad[...] = sums[0:128]
    bias_grad[...] = sums[128:129]


def join_kernel(*refs):
    out = refs[-1]
    at = 0
    for ref in refs[:-1]:
        size = min(ref.shape[0], out.shape[0] - at)
        out[pl.ds(at, size)] = ref[0:size]
        at += size


def join(name, size, *parts):
    return call(join_kernel, name, shape((size, 128, 128), BF), parts)


def body(features, weight, bias, block_values, block_rows, block_cols, block_counts, cotangent):
    slots = block_values.shape[2]
    row = lax.axis_index("row").astype(I32)
    place = jnp.stack(
        [lax.axis_index("col").astype(I32), row // (NC * NZ), row // NC % NZ, row % NC]
    )

    nodes = features.reshape(2, 128, 128)
    low, high = send_z(nodes, 3), send_z(nodes, -3)
    mine, words = fetch(nodes, block_rows, block_cols, place)
    near = join("join_near", 6, mine, low, high)
    from_up, from_down = send_z(near, 1), send_z(near, -1)
    up_near, down_near = send_y(near, 1), send_y(near, -1)
    other_near = swap(near, 1)
    rest = join("join_rest", 10, from_up, from_down)
    rest, up_near, down_near, other_near, words = lax.optimization_barrier(
        (rest, up_near, down_near, other_near, words)
    )
    up_rest, down_rest = send_y(rest, 1), send_y(rest, -1)
    far_near = send_y(up_near, 1)
    lists, totals, values = prepare(words, block_counts, block_values[0, 0])
    values = pltpu.with_memory_space_constraint(values, pltpu.VMEM)
    up_rest, down_rest, lists, totals = lax.optimization_barrier((up_rest, down_rest, lists, totals))
    far_rest = send_y(down_rest, -1)
    near_pieces = [near, rest, up_near, up_rest, down_near, down_rest]
    other_near = [other_near] + [swap(piece, 1) for piece in near_pieces[1:]]
    before = forward_near(lists, totals, values, near_pieces + other_near)
    far_near, far_rest, before = lax.optimization_barrier((far_near, far_rest, before))
    far_pieces = [far_near, far_rest]
    other_far = [swap(piece, 1) for piece in far_pieces]
    keep, send1, send2, send3 = forward_far(
        lists, totals, place, values, far_pieces + other_far, before
    )

    got = [send_x(send, step) for step, send in ((2, send2), (1, send1), (3, send3))]
    activated, message = layer(keep, got, weight, bias, cotangent)
    messages = [message] + [send_x(message, step) for step in MESSAGES[1:]]

    back_args = (lists, totals, place, values, messages)
    other = back(back_other_kernel, "back_other", shape((8192 + TERMS, 128), BF), *back_args)
    got = swap(other, 1)
    own = back(back_own_kernel, "back_own", shape((64, 128, 128), BF), *back_args)
    up, down, last, here, terms = call(
        sum_core_kernel,
        "sum_core",
        (
            shape((16, 128, 128), BF),
            shape((16, 128, 128), BF),
            shape((16, 128, 128), F32),
            shape((16, 128, 128), F32),
            shape((TERMS, 128), F32),
        ),
        (own, other, got),
    )
    from_up, from_down = send_y(up, 1), send_y(down, -1)
    for bit in (8, 4):
        terms = terms + swap(terms, bit)
    from_up, from_down, terms = lax.optimization_barrier((from_up, from_down, terms))
    up, down, short = call(
        sum_last_kernel,
        "sum_last",
        (shape((1024 + TERMS, 128), BF),) * 2 + (shape((TERMS, 128), BF),),
        (last, from_up, from_down, terms),
    )
    last_up, last_down = send_y(up, 1), send_y(down, -1)
    up, down, keep, terms = call(
        sum_y_kernel,
        "sum_y",
        (
            shape((6, 128, 128), BF),
            shape((4, 128, 128), BF),
            shape((6, 128, 128), F32),
            shape((TERMS, 128), F32),
        ),
        (here, from_up, from_down, last_up, last_down, short, swap(short, 32)),
    )
    up, down = send_z(up, 1), send_z(down, -1)
    got_terms = swap(terms, 2)
    up, down, got_terms = lax.optimization_barrier((up, down, got_terms))
    high, low, here = call(
        sum_z_kernel,
        "sum_z",
        (shape((2, 128, 128), BF),) * 2 + (shape((2, 128, 128), F32),),
        (keep, up, down),
    )
    high, low = send_z(high, 3), send_z(low, -3)
    scale = 1.0 / math.sqrt(features.shape[0] * NROW * NX)

    def end_kernel(*refs):
        sum_end_kernel(scale, *refs)

    feature_grad, weight_grad, bias_grad = call(
        end_kernel,
        "sum_end",
        (shape((256, 128), F32), shape((128, 128), F32), shape((1, 128), F32)),
        (here, high, low, terms, got_terms),
    )
    return (activated, feature_grad, weight_grad, bias_grad.reshape(128))


def solution(mesh):
    return jax.shard_map(
        body,
        mesh=mesh,
        in_specs=(
            P(("col", "row"), None),
            P(),
            P(),
            P("row", "col", None, None, None),
            P("row", "col", None),
            P("row", "col", None),
            P("row", "col"),
            P(("row", "col"), None),
        ),
        out_specs=(P(("row", "col"), None), P(("col", "row"), None), P(), P()),
        check_vma=False,
    )
```

```python
import math

import jax
import jax.numpy as jnp
import numpy as np
from jax import lax
from jax.experimental import pallas as pl
from jax.experimental.pallas import tpu as pltpu
from jax.sharding import PartitionSpec as P

BF = jnp.bfloat16
F32 = jnp.float32
I32 = jnp.int32
NY, NZ, NC, NX = 4, 8, 2, 4
NROW = NY * NZ * NC
STEP = 16
LONG = 32
LOAD = 16
GATHER_Z = (0, 5, 3, 7, 4, 2, 1, 6)
SCATTER_Z = (6, 1, 4, 7, 2, 0, 5, 3)
GATHER_Y = (0, 3, 1)
SCATTER_Y = (2, 1, 3, 0)
FAR_OTHER, FAR_OWN, OTHER, OWN = 0, 1, 2, 3
HIDDEN, TERMS = 256, 144
MESSAGES = (0, 1, 3, 2)

VMEM = pl.BlockSpec(memory_space=pltpu.VMEM)
SMEM = pl.BlockSpec(memory_space=pltpu.SMEM)
HBM = pl.BlockSpec(memory_space=pltpu.HBM)


def packed_order(order):
    return sum(order.index(n) << (3 * n) for n in range(max(order) + 1) if n in order)


def describe(rows, columns, place):
    slot = lax.broadcasted_iota(I32, rows.shape, 2)
    own = (((columns >> 1) ^ place[3]) & 1) ^ 1
    dz = ((columns >> 2) - place[2]) & (NZ - 1)
    dy = ((columns >> 5) - place[1]) & (NY - 1)

    def find(order, number):
        return (packed_order(order) >> (3 * number)) & 7

    far = dy == 2
    kind = own + jnp.where(far, 0, 2)
    gather = find(GATHER_Z, dz) * 2 + jnp.where(far, (1 - own) * 16, find(GATHER_Y, dy) * 16 + (1 - own) * 48)
    scatter = find(SCATTER_Z, dz) * 2 + find(SCATTER_Y, dy) * 16
    odd = columns & 1
    return kind | (slot << 2) | (rows << 11) | ((gather + odd) << 15) | ((scatter + odd) << 22)


def slot_of(word):
    return (word >> 2) & 511


def row_of(word):
    return (word >> 11) & 15


def gather_of(word):
    return (word >> 15) & 127


def scatter_of(word):
    return (word >> 22) & 127


def row_moves(dy=0, dz=0):
    moves = []
    for y in range(NY):
        for z in range(NZ):
            for c in range(NC):
                to = (((y + dy) % NY) * NZ + (z + dz) % NZ) * NC + c
                moves.append(((y * NZ + z) * NC + c, to))
    return moves


def send_y(value, step):
    return lax.ppermute(value, "row", row_moves(dy=step))


def send_z(value, step):
    return lax.ppermute(value, "row", row_moves(dz=step))


def swap(value, bit):
    return lax.ppermute(value, "row", [(i, i ^ bit) for i in range(NROW)])


def send_x(value, step):
    return lax.ppermute(value, "col", [(i, (i + step) % NX) for i in range(NX)])


def shape(dims, kind):
    return jax.ShapeDtypeStruct(dims, kind)


def call(kernel, name, outs, args, specs=None, out_specs=None, scratch=(), limit=16):
    single = not isinstance(outs, tuple)
    count = 1 if single else len(outs)
    out_specs = out_specs or [VMEM] * count
    return pl.pallas_call(
        kernel,
        out_shape=outs,
        in_specs=list(specs or [VMEM] * len(args)),
        out_specs=out_specs[0] if single else tuple(out_specs),
        scratch_shapes=list(scratch),
        compiler_params=pltpu.CompilerParams(vmem_limit_bytes=limit << 20),
        cost_estimate=pl.CostEstimate(flops=1, bytes_accessed=1, transcendentals=0),
        name=name,
    )(*args)


def fetch_kernel(features, rows, columns, place, mine, words, sem):
    copy = pltpu.make_async_copy(features, mine, sem)
    copy.start()
    words[...] = describe(rows[...], columns[...], place)
    copy.wait()


def in_hbm(value):
    return pltpu.with_memory_space_constraint(value, pltpu.HBM)


def fetch(features, rows, columns, place):
    return call(
        fetch_kernel,
        "fetch",
        (shape(features.shape, BF), shape(rows.shape, I32)),
        (in_hbm(features), rows, columns, place),
        specs=[HBM, VMEM, VMEM, SMEM],
        scratch=[pltpu.SemaphoreType.DMA],
    )


def prepare_kernel(words_in, count, values, lists, totals, held, words, sems):
    slots = values.shape[0]
    size = slots + STEP
    loads = slots // LOAD
    filled = count[0, 0]

    def load(c):
        part = pl.ds(c * LOAD, LOAD)
        return pltpu.make_async_copy(values.at[part], held.at[part], sems.at[c])

    all_words = pltpu.make_async_copy(words_in, words, sems.at[loads])
    all_words.start()
    for c in range(loads):
        pl.when(c * LOAD < filled)(lambda c=c: load(c).start())
    all_words.wait()

    def visit(k, found):
        word = words[0, 0, k]
        kind = jnp.where(k < filled, word & 3, 4)
        far = jnp.where(kind == FAR_OTHER, found[0], found[1])
        near = jnp.where(kind == OTHER, found[2], found[3])
        lists[kind * size + jnp.where(kind < OTHER, far, near)] = word
        return tuple(n + (kind == i).astype(I32) for i, n in enumerate(found))

    def group(g, found):
        for u in range(8):
            found = visit(g * 8 + u, found)
        return found

    found = lax.fori_loop(0, (filled + 7) // 8, group, (0, 0, 0, 0))
    spare = (8 << 11) | (64 << 22)
    for kind in range(4):
        for u in range(STEP):
            lists[kind * size + found[kind] + u] = spare
        totals[kind] = found[kind]
    for c in range(loads):
        pl.when(c * LOAD < filled)(lambda c=c: load(c).wait())


def prepare(words, count, values):
    slots = values.shape[0]
    return call(
        prepare_kernel,
        "prepare",
        (
            shape((5 * (slots + STEP),), I32),
            shape((4,), I32),
            pltpu.VMEM(values.shape, BF),
        ),
        (words, count, in_hbm(values)),
        specs=[VMEM, SMEM, HBM],
        out_specs=[SMEM, SMEM, VMEM],
        scratch=[pltpu.SMEM(words.shape, I32), pltpu.SemaphoreType.DMA((slots // LOAD + 1,))],
    )


def each_slot(kind, lists, totals, size, visit):
    def group(start, length):
        def step(g, carry):
            for u in range(length):
                visit(lists[kind * size + start + g * length + u])
            return carry

        return step

    count = totals[kind]
    long = count // LONG
    lax.fori_loop(0, long, group(0, LONG), 0)
    lax.fori_loop(0, (count - long * LONG + STEP - 1) // STEP, group(long * LONG, STEP), 0)


def lay(held, pieces):
    at = 0
    for piece in pieces:
        held[pl.ds(at, piece.shape[0])] = piece[...]
        at += piece.shape[0]


def forward_near_kernel(lists, totals, values, *rest):
    pieces, (out, held, total) = rest[:12], rest[12:]
    size = values.shape[0] + STEP
    lay(held, pieces)
    total[...] = jnp.zeros_like(total)

    def visit(word):
        total[row_of(word)] += jnp.dot(
            values[slot_of(word)], held[gather_of(word)], preferred_element_type=F32
        )

    each_slot(OWN, lists, totals, size, visit)
    each_slot(OTHER, lists, totals, size, visit)
    out[...] = total[0:8]


def forward_far_kernel(lists, totals, place, values, *rest):
    pieces, (before, keep, send1, send2, send3, held, total) = rest[:4], rest[4:]
    size = values.shape[0] + STEP
    lay(held, pieces)
    total[0:8] = before[...]
    total[8] = jnp.zeros_like(total[8])

    def visit(word):
        total[row_of(word)] += jnp.dot(
            values[slot_of(word)], held[gather_of(word)], preferred_element_type=F32
        )

    each_slot(FAR_OWN, lists, totals, size, visit)
    each_slot(FAR_OTHER, lists, totals, size, visit)
    x = place[0]
    keep[...] = total[pl.ds(2 * x, 2)]
    for step, send in ((1, send1), (2, send2), (3, send3)):
        send[...] = total[pl.ds(2 * lax.rem(x + step, NX), 2)].astype(BF)


def forward_near(lists, totals, values, pieces):
    return call(
        forward_near_kernel,
        "forward_near",
        shape((8, 128, 128), F32),
        (lists, totals, values, *pieces),
        specs=[SMEM, SMEM] + [VMEM] * 13,
        scratch=[pltpu.VMEM((96, 128, 128), BF), pltpu.VMEM((9, 128, 128), F32)]
    )


def forward_far(lists, totals, place, values, pieces, before):
    part = (2, 128, 128)
    return call(
        forward_far_kernel,
        "forward_far",
        (shape(part, F32), shape(part, BF), shape(part, BF), shape(part, BF)),
        (lists, totals, place, values, *pieces, before),
        specs=[SMEM, SMEM, SMEM] + [VMEM] * 6,
        scratch=[pltpu.VMEM((32, 128, 128), BF), pltpu.VMEM((9, 128, 128), F32)]
    )


def layer_kernel(keep, got1, got2, got3, weight, bias, cotangent, activated, message):
    total = keep[...] + got1[...].astype(F32) + got2[...].astype(F32) + got3[...].astype(F32)
    aggregated = total.reshape(256, 128).astype(BF)
    w = weight[...]
    pre = jnp.dot(aggregated, w, preferred_element_type=F32) + bias[...]
    root = math.sqrt(2.0 / math.pi)
    square = pre * pre
    tanh = jnp.tanh(root * (pre + 0.044715 * (pre * square)))
    cdf = 0.5 * (1.0 + tanh)
    activated[...] = (pre * cdf).astype(BF)
    slope = cdf + 0.5 * pre * (1.0 - tanh * tanh) * (root * (1.0 + 3.0 * 0.044715 * square))
    pre_grad = (cotangent[...].astype(F32) * slope).astype(BF)
    for half in range(2):
        message[half * 128 : half * 128 + 128] = lax.dot_general(
            w, pre_grad[half * 128 : half * 128 + 128], (((1,), (1,)), ((), ())),
            preferred_element_type=F32,
        ).astype(BF)
    message[HIDDEN : HIDDEN + 128] = lax.dot_general(
        aggregated, pre_grad, (((0,), (0,)), ((), ())), preferred_element_type=F32
    ).astype(BF)
    bias_term = jnp.sum(pre_grad.astype(F32), axis=0, keepdims=True)
    message[HIDDEN + 128 : HIDDEN + TERMS] = jnp.broadcast_to(bias_term, (TERMS - 128, 128)).astype(BF)


def layer(keep, got, weight, bias, cotangent):
    return call(
        layer_kernel,
        "layer",
        (shape((256, 128), BF), shape((HIDDEN + TERMS, 128), BF)),
        (keep, *got, weight, bias.reshape(1, 128), cotangent),
    )


def gather_hidden(place, messages, hidden):
    x = place[0]
    for step, part in zip(MESSAGES, messages):
        at = 2 * lax.rem(x + NX - step, NX)
        hidden[at] = part[0:128]
        hidden[at + 1] = part[128:256]
    hidden[8] = jnp.zeros_like(hidden[8])


def back_products(kinds, lists, totals, values, hidden, total):
    total[...] = jnp.zeros_like(total)

    def visit(word):
        total[scatter_of(word)] += jnp.dot(
            hidden[row_of(word)], values[slot_of(word)], preferred_element_type=F32
        )

    for kind in kinds:
        each_slot(kind, lists, totals, values.shape[0] + STEP, visit)


def back_other_kernel(lists, totals, place, values, m0, m1, m2, m3, out, hidden, total):
    gather_hidden(place, (m0, m1, m2, m3), hidden)
    back_products((FAR_OTHER, OTHER), lists, totals, values, hidden, total)
    out[0:8192] = total[0:64].reshape(8192, 128).astype(BF)
    rows = slice(HIDDEN, HIDDEN + TERMS)
    even = m0[rows].astype(F32) + m3[rows].astype(F32)
    odd = m1[rows].astype(F32) + m2[rows].astype(F32)
    out[8192 : 8192 + TERMS] = (even + odd).astype(BF)


def back_own_kernel(lists, totals, place, values, m0, m1, m2, m3, out, hidden, total):
    gather_hidden(place, (m0, m1, m2, m3), hidden)
    back_products((FAR_OWN, OWN), lists, totals, values, hidden, total)
    out[...] = total[0:64].astype(BF)


def back(kernel, name, out, lists, totals, place, values, messages):
    return call(
        kernel,
        name,
        out,
        (lists, totals, place, values, *messages),
        specs=[SMEM, SMEM, SMEM] + [VMEM] * 5,
        scratch=[pltpu.VMEM((9, 128, 128), BF), pltpu.VMEM((65, 128, 128), F32)],
    )


def add(*terms):
    total = terms[0].astype(F32)
    for term in terms[1:]:
        total = total + term.astype(F32)
    return total


def sum_core_kernel(own, mine, got, up, down, last, here, terms):
    def both(lo, hi):
        return add(own[lo:hi], got[lo * 128 : hi * 128].reshape(hi - lo, 128, 128))

    up[0:8] = both(0, 8).astype(BF)
    down[0:8] = both(8, 16).astype(BF)
    last[0:8] = both(16, 24)
    up[8:16] = both(24, 32).astype(BF)
    down[8:16] = both(32, 40).astype(BF)
    last[8:16] = both(40, 48)
    here[...] = both(48, 64)
    rows = slice(8192, 8192 + TERMS)
    terms[...] = add(mine[rows], got[rows])


def sum_last_kernel(last, from_up, from_down, terms, up, down, short):
    up[0:1024] = add(last[0:8], from_up[0:8]).reshape(1024, 128).astype(BF)
    down[0:1024] = add(last[8:16], from_down[0:8]).reshape(1024, 128).astype(BF)
    short[...] = terms[...].astype(BF)
    for message in (up, down):
        message[1024 : 1024 + TERMS] = terms[...].astype(BF)


def sum_y_kernel(here, from_up, from_down, last_up, last_down, short, got, up, down, keep, terms):
    first = add(here[0:8], from_down[8:16], last_up[0:1024].reshape(8, 128, 128))
    second = add(here[8:16], from_up[8:16], last_down[0:1024].reshape(8, 128, 128))
    up[...] = first[0:6].astype(BF)
    down[0:2] = first[6:8].astype(BF)
    down[2:4] = second[0:2].astype(BF)
    keep[...] = second[2:8]
    rows = slice(1024, 1024 + TERMS)
    terms[...] = add(short[...], got[...]) + add(last_up[rows], last_down[rows])


def sum_z_kernel(keep, up, down, high, low, here):
    here[...] = add(keep[0:2], up[2:4], down[0:2])
    low[...] = add(keep[2:4], up[0:2]).astype(BF)
    high[...] = add(keep[4:6], up[4:6], down[2:4]).astype(BF)


def sum_end_kernel(scale, here, high, low, terms, got, feature_grad, weight_grad, bias_grad):
    total = add(here[...], high[...], low[...])
    feature_grad[0:128] = total[0].T
    feature_grad[128:256] = total[1].T
    sums = (terms[...] + got[...]) * scale
    weight_grad[...] = sums[0:128]
    bias_grad[...] = sums[128:129]


def join_kernel(*refs):
    out = refs[-1]
    at = 0
    for ref in refs[:-1]:
        size = min(ref.shape[0], out.shape[0] - at)
        out[pl.ds(at, size)] = ref[0:size]
        at += size


def join(name, size, *parts):
    return call(join_kernel, name, shape((size, 128, 128), BF), parts)


def body(features, weight, bias, block_values, block_rows, block_cols, block_counts, cotangent):
    slots = block_values.shape[2]
    row = lax.axis_index("row").astype(I32)
    place = jnp.stack(
        [lax.axis_index("col").astype(I32), row // (NC * NZ), row // NC % NZ, row % NC]
    )

    nodes = features.reshape(2, 128, 128)
    low, high = send_z(nodes, 3), send_z(nodes, -3)
    mine, words = fetch(nodes, block_rows, block_cols, place)
    near = join("join_near", 6, mine, low, high)
    from_up, from_down = send_z(near, 1), send_z(near, -1)
    up_near, down_near = send_y(near, 1), send_y(near, -1)
    rest = join("join_rest", 10, from_up, from_down)
    rest, up_near, down_near, words = lax.optimization_barrier((rest, up_near, down_near, words))
    up_rest, down_rest = send_y(rest, 1), send_y(rest, -1)
    far_near = send_y(up_near, 1)
    lists, totals, values = prepare(words, block_counts, block_values[0, 0])
    values = pltpu.with_memory_space_constraint(values, pltpu.VMEM)
    up_rest, down_rest, lists, totals = lax.optimization_barrier((up_rest, down_rest, lists, totals))
    far_rest = send_y(down_rest, -1)
    near_pieces = [near, rest, up_near, up_rest, down_near, down_rest]
    other_near = [swap(piece, 1) for piece in near_pieces]
    before = forward_near(lists, totals, values, near_pieces + other_near)
    far_near, far_rest, before = lax.optimization_barrier((far_near, far_rest, before))
    far_pieces = [far_near, far_rest]
    other_far = [swap(piece, 1) for piece in far_pieces]
    keep, send1, send2, send3 = forward_far(
        lists, totals, place, values, far_pieces + other_far, before
    )

    got = [send_x(send, step) for step, send in ((2, send2), (1, send1), (3, send3))]
    activated, message = layer(keep, got, weight, bias, cotangent)
    messages = [message] + [send_x(message, step) for step in MESSAGES[1:]]

    back_args = (lists, totals, place, values, messages)
    other = back(back_other_kernel, "back_other", shape((8192 + TERMS, 128), BF), *back_args)
    got = swap(other, 1)
    own = back(back_own_kernel, "back_own", shape((64, 128, 128), BF), *back_args)
    up, down, last, here, terms = call(
        sum_core_kernel,
        "sum_core",
        (
            shape((16, 128, 128), BF),
            shape((16, 128, 128), BF),
            shape((16, 128, 128), F32),
            shape((16, 128, 128), F32),
            shape((TERMS, 128), F32),
        ),
        (own, other, got),
    )
    from_up, from_down = send_y(up, 1), send_y(down, -1)
    for bit in (8, 4):
        terms = terms + swap(terms, bit)
    from_up, from_down, terms = lax.optimization_barrier((from_up, from_down, terms))
    up, down, short = call(
        sum_last_kernel,
        "sum_last",
        (shape((1024 + TERMS, 128), BF),) * 2 + (shape((TERMS, 128), BF),),
        (last, from_up, from_down, terms),
    )
    last_up, last_down = send_y(up, 1), send_y(down, -1)
    up, down, keep, terms = call(
        sum_y_kernel,
        "sum_y",
        (
            shape((6, 128, 128), BF),
            shape((4, 128, 128), BF),
            shape((6, 128, 128), F32),
            shape((TERMS, 128), F32),
        ),
        (here, from_up, from_down, last_up, last_down, short, swap(short, 32)),
    )
    up, down = send_z(up, 1), send_z(down, -1)
    got_terms = swap(terms, 2)
    up, down, got_terms = lax.optimization_barrier((up, down, got_terms))
    high, low, here = call(
        sum_z_kernel,
        "sum_z",
        (shape((2, 128, 128), BF),) * 2 + (shape((2, 128, 128), F32),),
        (keep, up, down),
    )
    high, low = send_z(high, 3), send_z(low, -3)
    scale = 1.0 / math.sqrt(features.shape[0] * NROW * NX)

    def end_kernel(*refs):
        sum_end_kernel(scale, *refs)

    feature_grad, weight_grad, bias_grad = call(
        end_kernel,
        "sum_end",
        (shape((256, 128), F32), shape((128, 128), F32), shape((1, 128), F32)),
        (here, high, low, terms, got_terms),
    )
    return (activated, feature_grad, weight_grad, bias_grad.reshape(128))


def solution(mesh):
    return jax.shard_map(
        body,
        mesh=mesh,
        in_specs=(
            P(("col", "row"), None),
            P(),
            P(),
            P("row", "col", None, None, None),
            P("row", "col", None),
            P("row", "col", None),
            P("row", "col"),
            P(("row", "col"), None),
        ),
        out_specs=(P(("row", "col"), None), P(("col", "row"), None), P(), P()),
        check_vma=False,
    )
```
